256 devices in a mesh: group: 8 (over y, core), shard: 32 (over x, z).
Axes of the slice: x: 4, y: 4, z: 8, core: 2. Of those that a mesh axis runs over, the one named last changes fastest.
Arguments:
- query_states: bfloat16 [16384, 32, 1024], P(('group', 'shard')), may hold values from -6 to 6
- passage_states: bfloat16 [1024, 128, 1024], P(('group', 'shard')), may hold values from -6 to 6
- index_rows: bfloat16 [524288, 1024], P(('group', 'shard')), may hold values from -15 to 15
- weight: bfloat16 [1024, 1024], P('group'), may hold values from -0.1875 to 0.1875
- prev_weight: bfloat16 [1024, 1024], P('group'), may hold values from -0.1875 to 0.1875
- neg_owner: int32 [16384, 8, 1], P(('group', 'shard')), may hold values from 0 to 31; in each aligned block of 512 rows (0 to 511, 512 to 1023, ..., all dimensions but the last counted through in order) at most 32 rows name the same one
- neg_row: int32 [16384, 8], P(('group', 'shard')), may hold values from 0 to 2047
- positive: int32 [16384], P(('group', 'shard')), may hold values from 0 to 127
Outputs:
- grad_weight: float32 [1024, 1024], P('shard')
- query_loss: float32 [16384], P(('group', 'shard'))
- reencoded_document_embeddings: bfloat16 [1024, 1024], P(('group', 'shard'))
The draws below stay inside these ranges and needn't reach their ends.
Inputs may be any that keep to these rules, and one draw needn't show every extreme that they name: `neg_owner`: in the rows of one device no shard is named more than 32 times, a bound that some block reaches.
All inputs are finite; a program needn't handle non-finite values.
Results may differ from the reference program's by a relative error of at most 0.0065.
Values may be sent and summed in bfloat16 or wider, within the bound.
A program may use at most 64 MiB of HBM per device.

```python
import math
import jax
import jax.numpy as jnp
import numpy as np
from jax import lax

D = 1024
Q_DEV = 64
QLEN = 32
P_DEV = 4
PLEN = 128
NEG = 8
ROWS_DEV = 2048
CAP = 32
QUESTION_NUMBER = 16384
PASSAGES = 1024
ROWS = 524288
P_GROUP = 128
N_GROUP = 8
N_SHARD = 32


def draw_index_rows(key, part):
    key = jax.random.fold_in(key, 7)
    key_base = jax.random.fold_in(key, 0)
    entry_scale = 0.6 / math.sqrt(PLEN)
    values = entry_scale * jnp.clip(jax.random.normal(key_base, (ROWS, D), jnp.float32), -6.0, 6.0)
    return values.astype(jnp.bfloat16)


def place_ends(array, own_key, least, largest):
    shape = array.shape
    index_at = [jax.random.randint(jax.random.fold_in(own_key, axis), (), 0, shape[axis]) for axis in range(len(shape))]
    array = array.at[tuple(index_at)].set(least)
    longest = shape.index(max(shape))
    index_at[longest] = (index_at[longest] + 1) % shape[longest]
    return array.at[tuple(index_at)].set(largest)


def levels(key, dims, shards, smallest, top_value):
    gain, own = 1.0, jax.random.fold_in(key, 6)
    for position, parts in shards:
        draws = jnp.exp(jax.random.uniform(jax.random.fold_in(own, position), (parts,), jnp.float32, smallest / len(shards), top_value / len(shards)))
        gain = gain * jnp.repeat(draws, dims[position] // parts).reshape([-1 if axis == position else 1 for axis in range(len(dims))])
    return gain


def deal_out(own_key, own, number, rows, number_of, top, reach, slope):
    sequence = jax.random.permutation(own_key, number_of)
    packed, common = load_shares(number_of, rows * top, reach, slope, True), load_shares(number_of, rows * top, reach, slope, False)
    places = jnp.arange(number_of)

    def named(lengths, rotation):
        used = int((lengths > 0).sum())
        fixed = max(1, used // 4)
        moved = fixed + (places - fixed + rotation * (used - fixed)) % max(1, number_of - fixed)
        return jnp.zeros((number_of,), jnp.int32).at[sequence[jnp.where(places < fixed, places, moved)]].set(jnp.asarray(lengths, jnp.int32))

    lengths = jnp.where(number % 4 == 0, named(packed, number // 4), named(common, number - number // 4 - 1))
    mixed = jax.random.permutation(jax.random.fold_in(own, 3), number_of)
    donor, receiver = mixed[0:number_of // 2 * 2:2], mixed[1:number_of // 2 * 2:2]
    slack = jnp.minimum(lengths[donor] - 1, reach - lengths[receiver]) // 2
    slack = jnp.where((donor == sequence[0]) | (receiver == sequence[0]) | (lengths[receiver] == 0), 0, jnp.maximum(slack, 0))
    moved = jax.random.randint(jax.random.fold_in(own, 4), (number_of // 2,), 0, 1 << 20) % (slack + 1)
    lengths = lengths.at[donor].add(-moved).at[receiver].add(moved)
    members = jnp.searchsorted(jnp.cumsum(lengths), jnp.arange(rows * top), side="right").astype(jnp.int32)
    listing = members.reshape(top, rows).T
    listing = listing[jax.random.permutation(jax.random.fold_in(own, 1), rows)]
    rotation = jax.random.randint(jax.random.fold_in(own, 2), (rows, 1), 0, top)
    return jnp.take_along_axis(listing, (jnp.arange(top)[None, :] + rotation) % top, axis=1)


def load_shares(count, total, most, slope, full):
    portions = [(1 << 20) // math.isqrt(grade ** slope) + 1 for grade in range(1, count + 1)]
    largest = most if full else min(most, max(-(-total // count), total * portions[0] // sum(portions)))
    least = 1 if total - largest >= count - 1 else 0
    counts, surplus = [largest] + [least] * (count - 1), total - largest - least * (count - 1)
    while surplus > 0:
        free = [i for i in range(1, count) if counts[i] < largest] or [i for i in range(1, count) if counts[i] < most]
        pool, budget = sum([portions[i] for i in free]), surplus
        for i in free:
            addition = min(most - counts[i], max(1, budget * portions[i] // pool), surplus)
            counts[i] = counts[i] + addition
            surplus = surplus - addition
    return np.array(counts)


def scatter_about(stream_key, extent, scale, reach, cuts=(), kind=jnp.bfloat16):
    array = scale * jax.random.normal(stream_key, extent, jnp.float32)
    if cuts:
        array = array * levels(stream_key, extent, cuts, -0.22, 0.18)
    return jnp.clip(array, -reach, reach).astype(kind)


def setup_inputs(seed: int = 0) -> dict:
    seeds = jax.random.split(jax.random.key(seed), 9)
    query_states = scatter_about(seeds[0], (QUESTION_NUMBER, QLEN, D), 1.0, 6.0, ((0, 256),))
    passage_states = scatter_about(seeds[1], (PASSAGES, PLEN, D), 1.0, 6.0, ((0, 256),))
    index_rows = draw_index_rows(jax.random.fold_in(seeds[8], 71), 0)
    weight = scatter_about(seeds[3], (D, D), D ** -0.5, 0.1875, ((0, 8),))
    prev_weight = scatter_about(seeds[4], (D, D), D ** -0.5, 0.1875, ((0, 8),))
    neg_owner_keys = jax.random.split(jax.random.fold_in(seeds[5], 1), QUESTION_NUMBER * NEG // (Q_DEV * NEG))
    neg_owner_turns = jax.random.permutation(jax.random.fold_in(seeds[5], 3), QUESTION_NUMBER * NEG // (Q_DEV * NEG))
    neg_owner = jax.vmap(lambda own, number: deal_out(jax.random.fold_in(seeds[5], 2), own, number, Q_DEV * NEG, N_SHARD, 1, CAP, 2))(neg_owner_keys, neg_owner_turns).reshape((QUESTION_NUMBER, NEG, 1))
    neg_row = place_ends(jax.random.randint(seeds[6], (QUESTION_NUMBER, NEG), 0, ROWS_DEV), jax.random.fold_in(seeds[6], 1), 0, ROWS_DEV - 1).astype(jnp.int32)
    positive = place_ends(jax.random.randint(seeds[7], (QUESTION_NUMBER,), 0, P_DEV * N_SHARD), jax.random.fold_in(seeds[7], 1), 0, (P_DEV * N_SHARD) - 1).astype(jnp.int32)
    return dict(query_states=query_states, passage_states=passage_states, index_rows=index_rows, weight=weight, prev_weight=prev_weight, neg_owner=neg_owner, neg_row=neg_row, positive=positive)


logit_divisor = 0.05

def encode(states, matrix):
    item_count, seq_length, feat_width = states.shape
    flat_rows = states.reshape(item_count * seq_length, feat_width)
    hidden = jnp.tanh(jnp.dot(flat_rows, matrix, preferred_element_type=jnp.float32))
    return hidden.reshape(item_count, seq_length, feat_width)

def reference(query_states, passage_states, index_rows, weight, prev_weight, neg_owner, neg_row, positive):
    multiplier_coefficient = 1.0 / (logit_divisor * math.sqrt(QUESTION_NUMBER))

    def one_group(group_data):
        queries, passages, slab_rows, owners, pick_rows, labels = group_data
        reencoded_document_embeddings = lax.optimization_barrier(jnp.mean(encode(passages, prev_weight), axis=1)).astype(jnp.bfloat16)
        hidden = encode(queries, weight)
        question_embedding = lax.optimization_barrier(jnp.mean(hidden, axis=1)).astype(jnp.bfloat16)
        distractor_embeddings = jnp.take(slab_rows, (owners * ROWS_DEV + pick_rows).astype(jnp.int32), axis=0)
        within_minibatch_similarity = jnp.dot(question_embedding, reencoded_document_embeddings.T, preferred_element_type=jnp.float32) / logit_divisor
        distractor_similarity = jnp.einsum('mz,mfz->mf', question_embedding.astype(jnp.float32), distractor_embeddings.astype(jnp.float32)) / logit_divisor
        logits = jnp.concatenate([within_minibatch_similarity, distractor_similarity], axis=1)
        row_max = lax.optimization_barrier(jnp.max(logits, axis=1, keepdims=True))
        exp_terms = jnp.exp(logits - row_max)
        row_total = lax.optimization_barrier(jnp.sum(exp_terms, axis=1, keepdims=True))
        softmax_w = exp_terms / row_total
        label_hot = (jnp.arange(P_GROUP)[None, :] == labels[:, None]).astype(jnp.float32)
        picked = lax.optimization_barrier(jnp.sum(within_minibatch_similarity * label_hot, axis=1))
        loss_vec = jnp.log(row_total[:, 0]) + row_max[:, 0] - picked
        coeff_in = (softmax_w[:, :P_GROUP] - label_hot).astype(jnp.bfloat16)
        coeff_neg = softmax_w[:, P_GROUP:].astype(jnp.bfloat16)
        query_grad = jnp.dot(coeff_in, reencoded_document_embeddings, preferred_element_type=jnp.float32)
        query_grad = query_grad + jnp.einsum('qn,qnd->qd', coeff_neg.astype(jnp.float32), distractor_embeddings.astype(jnp.float32))
        query_grad = query_grad * multiplier_coefficient
        hidden_grad = ((1.0 - hidden * hidden) * (query_grad[:, None, :] / QLEN)).astype(jnp.bfloat16)
        partial_grad = jnp.dot(queries.reshape(-1, D).T, hidden_grad.reshape(-1, D), preferred_element_type=jnp.float32)
        return (partial_grad, loss_vec, reencoded_document_embeddings)
    group_data = (query_states.reshape(N_GROUP, N_SHARD * Q_DEV, QLEN, D), passage_states.reshape(N_GROUP, N_SHARD * P_DEV, PLEN, D), index_rows.reshape(N_GROUP, N_SHARD * ROWS_DEV, D), neg_owner.reshape(N_GROUP, N_SHARD * Q_DEV, NEG), neg_row.reshape(N_GROUP, N_SHARD * Q_DEV, NEG), positive.reshape(N_GROUP, N_SHARD * Q_DEV))
    grads, losses, fresh_all = lax.map(one_group, group_data)
    return (lax.optimization_barrier(jnp.sum(grads, axis=0)), losses.reshape(QUESTION_NUMBER), fresh_all.reshape(PASSAGES, D))
```

```python
import functools
import math

import jax
import jax.numpy as jnp
from jax import lax
from jax.experimental import pallas as pl
from jax.experimental.pallas import tpu as pltpu
from jax.sharding import PartitionSpec as P

MESH = pl.DeviceIdType.MESH
BF = jnp.bfloat16
F32 = jnp.float32

logit_divisor = 0.05

D = 1024
QD = 64
QL = 32
PD = 4
PL = 128
NEG = 8
ROWS = 2048
CAP = 32
NY, NC, NX, NZ = 4, 2, 4, 8
NG, NS = NY * NC, NX * NZ
TOK = QD * QL
SLOTS = NS * CAP
GRAD_SCALE = 1.0 / (logit_divisor * math.sqrt(QD * NS * NG))


def iota(shape, axis):
    return lax.broadcasted_iota(jnp.int32, shape, axis)


def to_column(row, n):
    eye = iota((n, n), 0) == iota((n, n), 1)
    return jnp.sum(jnp.where(eye, row, jnp.zeros_like(row)), axis=1, keepdims=True)


def to_row(column, n):
    eye = iota((n, n), 0) == iota((n, n), 1)
    return jnp.sum(jnp.where(eye, column, jnp.zeros_like(column)), axis=0, keepdims=True)


def kernel(
    owner_ref, row_ref, pos_ref, x_hbm, p_hbm, idx_hbm, w_hbm, pw_hbm,
    grad_ref, loss_ref, emb_ref,
    x_v, xt_v, p_v, idx_v, wp_v, ww_v,
    req_s, req_l, found, answer, mask_v,
    emb_f, emb_s, emb_l, e_v,
    d1_v, qv_f, qv_v, s_v, qg_v, hg_v,
    ex_s, ex_l, own_v, acc_a, acc_b, a_s, b_s, a_l, b_l,
    a2_s, b2_s, a2_l, b2_l, a2_o, b2_o, z_s, z_l, z_o, f_s, f_l,
    loc_sem, req_ss, req_rs, row_ss, row_rs, wp_ss, wp_rs, ww_ss, ww_rs,
    fp_ss, fw_ss, emb_ss, emb_rs, ex_ss, ex_rs, a_ss, a_rs, b_ss, b_rs,
    a2_ss, a2_rs, b2_ss, b2_rs, z_ss, z_rs, f_ss, f_rs,
):
    g, s = lax.axis_index("group"), lax.axis_index("shard")
    y, c = g // NC, g % NC
    x, z = s // NZ, s % NZ
    sib = y * NC + 1 - c

    def local(src, dst, k):
        return pltpu.make_async_copy(src, dst, loc_sem.at[k])

    def remote(src, dst, ss, rs, gg, sh):
        return pltpu.make_async_remote_copy(
            src_ref=src, dst_ref=dst, send_sem=ss, recv_sem=rs,
            device_id=(gg, sh), device_id_type=MESH,
        )

    def wait_in(dst, rs):
        remote(dst, dst, rs, rs, sib, s).wait_recv()

    def wait_out(src, ss):
        remote(src, src, ss, ss, sib, s).wait_send()

    barrier = pltpu.get_barrier_semaphore()

    @pl.loop(1, NS)
    def _(k):
        pl.semaphore_signal(barrier, inc=1, device_id=(g, (s + k) % NS), device_id_type=MESH)

    @pl.loop(1, NG)
    def _(k):
        pl.semaphore_signal(barrier, inc=1, device_id=((g + k) % NG, s), device_id_type=MESH)

    local_copies = [
        local(idx_hbm, idx_v, 0),
        local(pw_hbm, wp_v.at[g], 1),
        local(w_hbm, ww_v.at[g], 2),
        local(x_hbm, x_v, 3),
        local(p_hbm, p_v, 4),
    ]
    for copy in local_copies:
        copy.start()

    owners, rows = owner_ref[...], row_ref[...]
    lane = iota((QD, 128), 1)
    lower = (iota((QD, QD), 0) > iota((QD, QD), 1)).astype(F32).astype(BF)
    slot_lane = iota((QD, SLOTS), 1)
    base = jnp.zeros((1, 128), F32)
    mask = jnp.zeros((QD, SLOTS), F32)
    requests = jnp.zeros((128, 128), F32)
    for n in range(NEG):
        owner = owners[:, n : n + 1]
        hot = (lane == owner).astype(F32)
        before = jnp.dot(lower, hot.astype(BF), preferred_element_type=F32) + base
        rank = jnp.sum(hot * before, axis=1, keepdims=True).astype(jnp.int32)
        base = base + jnp.sum(hot, axis=0, keepdims=True)
        mask = mask + (slot_lane == owner * CAP + rank).astype(F32)
        row = rows[:, n : n + 1]
        here = lane == rank + (s % 4) * CAP
        high = jnp.where(here, row // 16, 0).astype(F32).astype(BF)
        low = jnp.where(here, row % 16, 0).astype(F32).astype(BF)
        hot_t = hot.T.astype(BF)
        requests = requests + (
            16.0 * jnp.dot(hot_t, high, preferred_element_type=F32)
            + jnp.dot(hot_t, low, preferred_element_type=F32)
        )
    mask_v[...] = mask
    for o in range(NS):
        req_s[o] = requests[o : o + 1, :]

    pl.semaphore_wait(barrier, NS - 1 + NG - 1)

    @pl.loop(1, NS)
    def _(k):
        o = (s + k) % NS
        remote(req_s.at[o], req_l.at[s], req_ss.at[o], req_rs.at[s], g, o).start()

    req_l[s] = req_s[s]

    for hbm, buf, ss, rs in ((pw_hbm, wp_v, wp_ss, wp_rs), (w_hbm, ww_v, ww_ss, ww_rs)):

        @pl.loop(1, NY)
        def _(k):
            peer = ((y + k) % NY) * NC + c
            remote(hbm, buf.at[g], ss.at[k], rs.at[g], peer, s).start()

        remote(hbm, buf.at[g], ss.at[0], rs.at[g], sib, s).start()

    @pl.loop(1, NS)
    def _(k):
        o = (s + k) % NS
        wait_in(req_l.at[o], req_rs.at[o])

    local_copies[0].wait()
    row_lane = iota((128, ROWS), 1)

    @pl.loop(0, NX)
    def _(i):
        xx = (x + 1 + i) % NX
        hots = []
        for half in range(NZ // 4):
            first = xx * NZ + half * 4
            ids = req_l[first] + req_l[first + 1] + req_l[first + 2] + req_l[first + 3]
            column = to_column(ids, 128).astype(jnp.int32)
            hots.append((row_lane == column).astype(F32).astype(BF))
        hot = jnp.concatenate(hots, axis=0)
        got = jnp.dot(hot, idx_v[...], preferred_element_type=F32).astype(BF)
        found[pl.ds(xx * NZ, NZ)] = got.reshape(NZ, CAP, D)

        @pl.loop(0, NZ)
        def _(k):
            r = xx * NZ + (z + 1 + k) % NZ

            @pl.when(r != s)
            def _():
                remote(found.at[r], answer.at[s], row_ss.at[r], row_rs.at[s], g, r).start()

    answer[s] = found[s]

    local_copies[3].wait()

    @pl.loop(0, TOK // 256)
    def _(i):
        at = pl.multiple_of(i * 256, 256)
        xt_v[:, pl.ds(at, 256)] = x_v[pl.ds(at, 256), :].T

    def gather_rest(buf, rs, fs):
        @pl.loop(1, NY)
        def _(k):
            peer = ((y + k) % NY) * NC + c
            wait_in(buf.at[peer], rs.at[peer])
            remote(buf.at[peer], buf.at[peer], fs.at[k], rs.at[peer], sib, s).start()

        @pl.loop(0, NY)
        def _(k):
            peer = k * NC + 1 - c
            wait_in(buf.at[peer], rs.at[peer])

    local_copies[1].wait()
    local_copies[4].wait()
    gather_rest(wp_v, wp_rs, fp_ss)
    for i in range(PD // 2):
        hidden = jnp.tanh(
            jnp.dot(
                p_v[i * 2 * PL : (i + 1) * 2 * PL, :],
                wp_v[...].reshape(D, D),
                preferred_element_type=F32,
            )
        )
        for j in range(2):
            mean = jnp.sum(hidden[j * PL : (j + 1) * PL], axis=0, keepdims=True) * (1.0 / PL)
            p = i * 2 + j
            for b in range(8):
                emb_f[b * PD + p : b * PD + p + 1, :] = mean[:, b * 128 : (b + 1) * 128]
    emb = emb_f[...].astype(BF)
    emb_s[...] = emb
    emb_l[s] = emb
    for b in range(8):
        emb_ref[:, b * 128 : (b + 1) * 128] = emb_f[b * PD : (b + 1) * PD, :].astype(BF)

    @pl.loop(1, NS)
    def _(k):
        o = (s + k) % NS
        remote(emb_s, emb_l.at[s], emb_ss.at[o], emb_rs.at[s], g, o).start()

    local_copies[2].wait()
    gather_rest(ww_v, ww_rs, fw_ss)

    @pl.loop(0, TOK // 256)
    def _(i):
        at = pl.multiple_of(i * 256, 256)
        hidden = jnp.tanh(
            jnp.dot(x_v[pl.ds(at, 256), :], ww_v[...].reshape(D, D), preferred_element_type=F32)
        )
        d1_v[pl.ds(at, 256), :] = 1.0 - hidden * hidden
        q_at = pl.multiple_of(i * 8, 8)
        qv_f[pl.ds(q_at, 8), :] = jnp.sum(hidden.reshape(8, QL, D), axis=1) * (1.0 / QL)

    qv_v[...] = qv_f[...].astype(BF)

    @pl.loop(1, NS)
    def _(k):
        o = (s + k) % NS
        wait_in(emb_l.at[o], emb_rs.at[o])

    pieces = emb_l[...].reshape(NS * 32, 128)
    to_passage, from_piece = iota((128, NS * 32), 0), iota((128, NS * 32), 1)
    for b in range(8):
        pick = (from_piece == (to_passage // PD) * 32 + b * PD + to_passage % PD)
        e_v[:, b * 128 : (b + 1) * 128] = jnp.dot(
            pick.astype(F32).astype(BF), pieces, preferred_element_type=F32
        ).astype(BF)

    nt = (((1,), (1,)), ((), ()))
    in_logits = (
        lax.dot_general(qv_v[...], e_v[...], nt, preferred_element_type=F32) / logit_divisor
    )

    @pl.loop(0, NX)
    def _(i):
        xx = (x + 2 * NX - 1 - i) % NX

        @pl.loop(0, NZ)
        def _(k):
            o = xx * NZ + (z + NZ + NZ - 1 - k) % NZ

            @pl.when(o != s)
            def _():
                wait_in(answer.at[o], row_rs.at[o])

        got = answer[pl.ds(xx * NZ, NZ)].reshape(NZ * CAP, D)
        s_v[:, pl.ds(pl.multiple_of(xx * NZ * CAP, NZ * CAP), NZ * CAP)] = lax.dot_general(
            qv_v[...], got, nt, preferred_element_type=F32
        )

    named = mask_v[...] > 0.5
    neg_logits = jnp.where(named, s_v[...] / logit_divisor, -jnp.inf)
    top = jnp.maximum(
        jnp.max(in_logits, axis=1, keepdims=True), jnp.max(neg_logits, axis=1, keepdims=True)
    )
    in_exp = jnp.exp(in_logits - top)
    neg_exp = jnp.where(named, jnp.exp(neg_logits - top), 0.0)
    total = jnp.sum(in_exp, axis=1, keepdims=True) + jnp.sum(neg_exp, axis=1, keepdims=True)
    label = (iota((QD, 128), 1) == to_column(pos_ref[...].astype(F32), QD).astype(jnp.int32))
    label = label.astype(F32)
    picked = jnp.sum(in_logits * label, axis=1, keepdims=True)
    loss_ref[...] = to_row(jnp.log(total) + top - picked, QD)
    coeff_in = (in_exp / total - label).astype(BF)
    coeff_neg = (neg_exp / total).astype(BF)
    query_grad = jnp.dot(coeff_in, e_v[...], preferred_element_type=F32) + jnp.dot(
        coeff_neg, answer[...].reshape(SLOTS, D), preferred_element_type=F32
    )
    qg_v[...] = query_grad * GRAD_SCALE * (1.0 / QL)

    @pl.loop(0, QD // 8)
    def _(i):
        q_at = pl.multiple_of(i * 8, 8)
        grads = qg_v[pl.ds(q_at, 8), :]
        for j in range(8):
            at = pl.multiple_of(i * 256 + j * QL, QL)
            value = (d1_v[pl.ds(at, QL), :] * grads[j : j + 1, :]).astype(BF)
            hg_v[0, pl.ds(at, QL), :] = value[:, : D // 2]
            hg_v[1, pl.ds(at, QL), :] = value[:, D // 2 :]

    def finish(i):
        xx = (x + 1 + i) % NX
        wait_in(ex_l.at[i], ex_rs.at[i])
        both = own_v[i % 2] + ex_l[i].astype(F32)
        both = both.reshape(NZ, 2, 16, D // 2)
        part_a = both[:, 0].reshape(NZ * 16, D // 2)
        part_b = both[:, 1].reshape(NZ * 16, D // 2)
        acc_b[xx] = part_b
        b_s[xx] = part_b.astype(BF)
        for k in range(NY):
            piece = part_a[:, k * 128 : (k + 1) * 128]
            acc_a[k, xx] = piece
            a_s[k, xx] = piece.astype(BF)

        @pl.when(i < NX - 1)
        def _():
            remote(b_s.at[xx], b_l.at[i], b_ss.at[i], b_rs.at[i], g, xx * NZ + z).start()

        @pl.loop(1, NY)
        def _(k):
            yy = (y + k) % NY
            remote(
                a_s.at[yy, xx], a_l.at[k - 1, xx], a_ss.at[k - 1, i], a_rs.at[k - 1, i],
                yy * NC + c, s,
            ).start()

    @pl.loop(0, NX)
    def _(i):
        xx = (x + 1 + i) % NX
        left = xt_v[pl.ds(pl.multiple_of(xx * 256, 256), 256), :]
        ex_s[i] = jnp.dot(left, hg_v[1 - c], preferred_element_type=F32).astype(BF)
        remote(ex_s.at[i], ex_l.at[i], ex_ss.at[i], ex_rs.at[i], sib, s).start()

        @pl.when(i > 0)
        def _():
            finish(i - 1)

        own_v[i % 2] = jnp.dot(left, hg_v[c], preferred_element_type=F32)

    finish(NX - 1)

    @pl.loop(0, NX)
    def _(i):
        xx = (x + 1 + i) % NX
        part = acc_a[y, xx]
        for k in range(1, NY):
            wait_in(a_l.at[k - 1, xx], a_rs.at[k - 1, i])
            part = part + a_l[k - 1, xx].astype(F32)

        @pl.when(i < NX - 1)
        def _():
            a2_s[i] = part.astype(BF)
            remote(a2_s.at[i], a2_l.at[i], a2_ss.at[i], a2_rs.at[i], g, xx * NZ + z).start()

        @pl.when(i == NX - 1)
        def _():
            a2_o[...] = part

    part_b = acc_b[x]
    for k in range(NX - 1):
        wait_in(b_l.at[k], b_rs.at[k])
        part_b = part_b + b_l[k].astype(F32)
    for k in range(NY):
        piece = part_b[:, k * 128 : (k + 1) * 128]
        b2_o[k] = piece
        b2_s[k] = piece.astype(BF)

    @pl.loop(1, NY)
    def _(k):
        yy = (y + k) % NY
        remote(b2_s.at[yy], b2_l.at[k - 1], b2_ss.at[k - 1], b2_rs.at[k - 1], yy * NC + c, s).start()

    part_a = a2_o[...]
    for k in range(NX - 1):
        wait_in(a2_l.at[k], a2_rs.at[k])
        part_a = part_a + a2_l[k].astype(F32)
    part_b = b2_o[y]
    for k in range(NY - 1):
        wait_in(b2_l.at[k], b2_rs.at[k])
        part_b = part_b + b2_l[k].astype(F32)
    part_a = part_a.reshape(NZ, 16, 128)
    part_b = part_b.reshape(NZ, 16, 128)
    z_o[:, 0:16, :] = part_a
    z_o[:, 16:32, :] = part_b
    z_s[...] = z_o[...].astype(BF)

    @pl.loop(1, NZ)
    def _(k):
        zz = (z + k) % NZ
        remote(z_s.at[zz], z_l.at[k - 1], z_ss.at[k - 1], z_rs.at[k - 1], g, x * NZ + zz).start()

    total_part = z_o[z]
    for k in range(NZ - 1):
        wait_in(z_l.at[k], z_rs.at[k])
        total_part = total_part + z_l[k].astype(F32)

    f_s[...] = total_part
    f_l[g] = total_part

    @pl.loop(1, NG)
    def _(k):
        gg = (g + k) % NG
        remote(f_s, f_l.at[g], f_ss.at[k], f_rs.at[g], gg, s).start()

    @pl.loop(1, NG)
    def _(k):
        gg = (g + k) % NG
        wait_in(f_l.at[gg], f_rs.at[gg])

    for yy in range(NY):
        for cc in range(NC):
            at = (cc * NY + yy) * 128
            grad_ref[:, at : at + 128] = f_l[yy * NC + cc]

    @pl.loop(1, NS)
    def _(k):
        o = (s + k) % NS
        wait_out(req_s.at[o], req_ss.at[o])
        wait_out(found.at[o], row_ss.at[o])
        wait_out(emb_s, emb_ss.at[o])

    for buf, ss, fs in ((wp_v, wp_ss, fp_ss), (ww_v, ww_ss, fw_ss)):

        @pl.loop(0, NY)
        def _(k):
            wait_out(buf.at[g], ss.at[k])

        @pl.loop(1, NY)
        def _(k):
            wait_out(buf.at[((y + k) % NY) * NC + c], fs.at[k])

    @pl.loop(0, NX)
    def _(i):
        wait_out(ex_s.at[i], ex_ss.at[i])

        @pl.loop(0, NY - 1)
        def _(k):
            wait_out(a_s.at[0, 0], a_ss.at[k, i])

    @pl.loop(0, NX - 1)
    def _(i):
        wait_out(b_s.at[i], b_ss.at[i])
        wait_out(a2_s.at[i], a2_ss.at[i])

    @pl.loop(0, NY - 1)
    def _(i):
        wait_out(b2_s.at[i], b2_ss.at[i])

    @pl.loop(0, NZ - 1)
    def _(i):
        wait_out(z_s.at[i], z_ss.at[i])

    @pl.loop(1, NG)
    def _(k):
        wait_out(f_s, f_ss.at[k])


def shards(
    query_states, passage_states, index_rows, weight, prev_weight, neg_owner, neg_row, positive
):
    vmem = pl.BlockSpec(memory_space=pltpu.VMEM)
    hbm = pl.BlockSpec(memory_space=pl.ANY)
    dma = pltpu.SemaphoreType.DMA
    half = D // 2
    scratch = [
        pltpu.VMEM((TOK, D), BF),
        pltpu.VMEM((D, TOK), BF),
        pltpu.VMEM((PD * PL, D), BF),
        pltpu.VMEM((ROWS, D), BF),
        pltpu.VMEM((NG, D // NG, D), BF),
        pltpu.VMEM((NG, D // NG, D), BF),
        pltpu.VMEM((NS, 1, 128), F32),
        pltpu.VMEM((NS, 1, 128), F32),
        pltpu.VMEM((NS, CAP, D), BF),
        pltpu.VMEM((NS, CAP, D), BF),
        pltpu.VMEM((QD, SLOTS), F32),
        pltpu.VMEM((32, 128), F32),
        pltpu.VMEM((32, 128), BF),
        pltpu.VMEM((NS, 32, 128), BF),
        pltpu.VMEM((NS * PD, D), BF),
        pltpu.VMEM((TOK, D), F32),
        pltpu.VMEM((QD, D), F32),
        pltpu.VMEM((QD, D), BF),
        pltpu.VMEM((QD, SLOTS), F32),
        pltpu.VMEM((QD, D), F32),
        pltpu.VMEM((2, TOK, half), BF),
        pltpu.VMEM((NX, 256, half), BF),
        pltpu.VMEM((NX, 256, half), BF),
        pltpu.VMEM((2, 256, half), F32),
        pltpu.VMEM((NY, NX, 128, 128), F32),
        pltpu.VMEM((NX, 128, half), F32),
        pltpu.VMEM((NY, NX, 128, 128), BF),
        pltpu.VMEM((NX, 128, half), BF),
        pltpu.VMEM((NY - 1, NX, 128, 128), BF),
        pltpu.VMEM((NX - 1, 128, half), BF),
        pltpu.VMEM((NX - 1, 128, 128), BF),
        pltpu.VMEM((NY, 128, 128), BF),
        pltpu.VMEM((NX - 1, 128, 128), BF),
        pltpu.VMEM((NY - 1, 128, 128), BF),
        pltpu.VMEM((128, 128), F32),
        pltpu.VMEM((NY, 128, 128), F32),
        pltpu.VMEM((NZ, 32, 128), BF),
        pltpu.VMEM((NZ - 1, 32, 128), BF),
        pltpu.VMEM((NZ, 32, 128), F32),
        pltpu.VMEM((32, 128), F32),
        pltpu.VMEM((NG, 32, 128), F32),
        dma((5,)),
        dma((NS,)), dma((NS,)),
        dma((NS,)), dma((NS,)),
        dma((NY,)), dma((NG,)),
        dma((NY,)), dma((NG,)),
        dma((NY,)), dma((NY,)),
        dma((NS,)), dma((NS,)),
        dma((NX,)), dma((NX,)),
        dma((NY - 1, NX)), dma((NY - 1, NX)),
        dma((NX - 1,)), dma((NX - 1,)),
        dma((NX - 1,)), dma((NX - 1,)),
        dma((NY - 1,)), dma((NY - 1,)),
        dma((NZ - 1,)), dma((NZ - 1,)),
        dma((NG,)), dma((NG,)),
    ]
    grad, loss, emb = pl.pallas_call(
        kernel,
        out_shape=(
            jax.ShapeDtypeStruct((D // NS, D), F32),
            jax.ShapeDtypeStruct((1, QD), F32),
            jax.ShapeDtypeStruct((PD, D), BF),
        ),
        in_specs=[vmem] * 3 + [hbm] * 5,
        out_specs=(vmem, vmem, vmem),
        scratch_shapes=scratch,
        compiler_params=pltpu.CompilerParams(
            collective_id=0, has_side_effects=True, vmem_limit_bytes=60 << 20
        ),
        cost_estimate=pl.CostEstimate(
            flops=16 * 2**30, bytes_accessed=12 * 2**20, transcendentals=3 * 2**20
        ),
        name="retriever_step",
    )(
        neg_owner.reshape(QD, NEG),
        neg_row,
        positive.reshape(1, QD),
        query_states.reshape(TOK, D),
        passage_states.reshape(PD * PL, D),
        index_rows,
        weight,
        prev_weight,
    )
    return grad, loss.reshape(QD), emb


def solution(mesh):
    return jax.shard_map(
        shards,
        mesh=mesh,
        in_specs=(
            P(("group", "shard"), None, None),
            P(("group", "shard"), None, None),
            P(("group", "shard"), None),
            P("group", None),
            P("group", None),
            P(("group", "shard"), None, None),
            P(("group", "shard"), None),
            P(("group", "shard")),
        ),
        out_specs=(P("shard", None), P(("group", "shard")), P(("group", "shard"), None)),
        check_vma=False,
    )
```

```python
import functools
import math

import jax
import jax.numpy as jnp
from jax import lax
from jax.experimental import pallas as pl
from jax.experimental.pallas import tpu as pltpu
from jax.sharding import PartitionSpec as P

MESH = pl.DeviceIdType.MESH
BF = jnp.bfloat16
F32 = jnp.float32

logit_divisor = 0.05

D = 1024
QD = 64
QL = 32
PD = 4
PL = 128
NEG = 8
ROWS = 2048
CAP = 32
NY, NC, NX, NZ = 4, 2, 4, 8
NG, NS = NY * NC, NX * NZ
TOK = QD * QL
SLOTS = NS * CAP
RA, RB = 5 * 32, 3 * 32
GRAD_SCALE = 1.0 / (logit_divisor * math.sqrt(QD * NS * NG))


def iota(shape, axis):
    return lax.broadcasted_iota(jnp.int32, shape, axis)


def to_column(row, n):
    eye = iota((n, n), 0) == iota((n, n), 1)
    return jnp.sum(jnp.where(eye, row, jnp.zeros_like(row)), axis=1, keepdims=True)


def to_row(column, n):
    eye = iota((n, n), 0) == iota((n, n), 1)
    return jnp.sum(jnp.where(eye, column, jnp.zeros_like(column)), axis=0, keepdims=True)


def kernel(
    owner_hbm, row_hbm, pos_hbm, x_hbm, p_hbm, idx_hbm, w_hbm, pw_hbm,
    grad_ref, loss_ref, emb_ref,
    owner_ref, row_ref, pos_ref, x_v, xt_v, p_v, idx_v, wp_v, ww_v,
    req_s, req_l, found, answer, mask_v,
    emb_f, emb_s, emb_l, e_v,
    d1_v, qv_f, qv_v, s_v, qg_v, hg_v,
    ex_s, ex_l, own_v, acc_a, acc_b, a_s, b_s, a_l, b_l,
    a2_s, b2_s, a2_l, b2_l, a2_o, b2_o, z_s, z_l, z_o, f_s, f_l,
    loc_sem, req_ss, req_rs, row_ss, row_rs, wp_ss, wp_rs, ww_ss, ww_rs,
    fp_ss, fw_ss, emb_ss, emb_rs, line_ss, line_rs, ex_ss, ex_rs, a_ss, a_rs, b_ss, b_rs,
    a2_ss, a2_rs, b2_ss, b2_rs, z_ss, z_rs, f_ss, f_rs,
):
    g, s = lax.axis_index("group"), lax.axis_index("shard")
    y, c = g // NC, g % NC
    x, z = s // NZ, s % NZ
    sib = y * NC + 1 - c

    def local(src, dst, k):
        return pltpu.make_async_copy(src, dst, loc_sem.at[k])

    def remote(src, dst, ss, rs, gg, sh):
        return pltpu.make_async_remote_copy(
            src_ref=src, dst_ref=dst, send_sem=ss, recv_sem=rs,
            device_id=(gg, sh), device_id_type=MESH,
        )

    def wait_in(dst, rs):
        remote(dst, dst, rs, rs, sib, s).wait_recv()

    def wait_out(src, ss):
        remote(src, src, ss, ss, sib, s).wait_send()

    nt = (((1,), (1,)), ((), ()))

    small_copies = [
        local(owner_hbm, owner_ref, 5),
        local(row_hbm, row_ref, 6),
        local(pos_hbm, pos_ref, 7),
    ]
    for copy in small_copies:
        copy.start()

    barrier = pltpu.get_barrier_semaphore()

    @pl.loop(1, NS)
    def _(k):
        pl.semaphore_signal(barrier, inc=1, device_id=(g, (s + k) % NS), device_id_type=MESH)

    @pl.loop(1, NG)
    def _(k):
        pl.semaphore_signal(barrier, inc=1, device_id=((g + k) % NG, s), device_id_type=MESH)

    local_copies = [
        local(idx_hbm, idx_v, 0),
        local(pw_hbm, wp_v.at[g], 1),
        local(w_hbm, ww_v.at[g], 2),
        local(x_hbm, x_v, 3),
        local(p_hbm, p_v, 4),
    ]
    for copy in local_copies:
        copy.start()

    for copy in small_copies:
        copy.wait()
    upper = (iota((QD, QD), 0) < iota((QD, QD), 1)).astype(F32).astype(BF)
    base = jnp.zeros((NS, 1), F32)
    requests = jnp.zeros((NS, 128), F32)
    slots = []
    for n in range(NEG):
        owner = owner_ref[n]
        hot = (iota((NS, QD), 0) == owner).astype(F32)
        hot_bf = hot.astype(BF)
        before = jnp.dot(hot_bf, upper, preferred_element_type=F32) + base
        rank = jnp.sum(hot * before, axis=0, keepdims=True).astype(jnp.int32)
        base = base + jnp.sum(hot, axis=1, keepdims=True)
        slots.append((owner * CAP + rank).astype(F32))
        row = row_ref[n : n + 1, :]
        here = iota((128, QD), 0) == rank + (s % 4) * CAP
        high = jnp.where(here, row // 16, 0).astype(F32).astype(BF)
        low = jnp.where(here, row % 16, 0).astype(F32).astype(BF)
        requests = requests + (
            16.0 * lax.dot_general(hot_bf, high, nt, preferred_element_type=F32)
            + lax.dot_general(hot_bf, low, nt, preferred_element_type=F32)
        )
    for o in range(NS):
        req_s[o] = requests[o : o + 1, :]

    pl.semaphore_wait(barrier, NS - 1 + NG - 1)

    @pl.loop(1, NS)
    def _(k):
        o = (s + k) % NS
        remote(req_s.at[o], req_l.at[s], req_ss.at[o], req_rs.at[s], g, o).start()

    req_l[s] = req_s[s]

    for hbm, buf, ss, rs in ((pw_hbm, wp_v, wp_ss, wp_rs), (w_hbm, ww_v, ww_ss, ww_rs)):

        @pl.loop(1, NY)
        def _(k):
            peer = ((y + k) % NY) * NC + c
            remote(hbm, buf.at[g], ss.at[k], rs.at[g], peer, s).start()

        remote(hbm, buf.at[g], ss.at[0], rs.at[g], sib, s).start()

    local_copies[0].wait()
    row_lane = iota((128, ROWS), 1)

    def send_rows(i):
        xx = (x + i) % NX

        @pl.loop(0, NZ)
        def _(k):
            r = xx * NZ + (z + 1 + k) % NZ

            @pl.when(r != s)
            def _():
                remote(found.at[r], answer.at[s], row_ss.at[r], row_rs.at[s], g, r).start()

    @pl.loop(0, NX)
    def _(i):
        xx = (x + i) % NX

        @pl.loop(0, NZ)
        def _(k):
            r = xx * NZ + (z + 1 + k) % NZ

            @pl.when(r != s)
            def _():
                wait_in(req_l.at[r], req_rs.at[r])

        hots = []
        for half in range(NZ // 4):
            first = xx * NZ + half * 4
            ids = req_l[first] + req_l[first + 1] + req_l[first + 2] + req_l[first + 3]
            column = to_column(ids, 128).astype(jnp.int32)
            hots.append((row_lane == column).astype(F32).astype(BF))
        hot = jnp.concatenate(hots, axis=0)
        got = jnp.dot(hot, idx_v[...], preferred_element_type=F32).astype(BF)
        found[pl.ds(xx * NZ, NZ)] = got.reshape(NZ, CAP, D)

        @pl.when(i < NX // 2)
        def _():
            send_rows(i)

    answer[s] = found[s]

    slot_lane = iota((QD, SLOTS), 1)
    mask = jnp.zeros((QD, SLOTS), F32)
    for n in range(NEG):
        mask = mask + (slot_lane == to_column(slots[n], QD).astype(jnp.int32)).astype(F32)
    mask_v[...] = mask

    local_copies[3].wait()

    @pl.loop(0, TOK // 256)
    def _(i):
        at = pl.multiple_of(i * 256, 256)
        xt_v[:, pl.ds(at, 256)] = x_v[pl.ds(at, 256), :].T

    def gather_rest(buf, rs, fs):
        @pl.loop(1, NY)
        def _(k):
            peer = ((y + k) % NY) * NC + c
            wait_in(buf.at[peer], rs.at[peer])
            remote(buf.at[peer], buf.at[peer], fs.at[k], rs.at[peer], sib, s).start()

        @pl.loop(0, NY)
        def _(k):
            peer = k * NC + 1 - c
            wait_in(buf.at[peer], rs.at[peer])

    local_copies[1].wait()
    local_copies[4].wait()
    gather_rest(wp_v, wp_rs, fp_ss)
    for i in range(PD // 2):
        hidden = jnp.tanh(
            jnp.dot(
                p_v[i * 2 * PL : (i + 1) * 2 * PL, :],
                wp_v[...].reshape(D, D),
                preferred_element_type=F32,
            )
        )
        for j in range(2):
            mean = jnp.sum(hidden[j * PL : (j + 1) * PL], axis=0, keepdims=True) * (1.0 / PL)
            p = i * 2 + j
            for b in range(8):
                emb_f[b * PD + p : b * PD + p + 1, :] = mean[:, b * 128 : (b + 1) * 128]
    emb = emb_f[...].astype(BF)
    emb_s[...] = emb
    emb_l[s] = emb
    for b in range(8):
        emb_ref[:, b * 128 : (b + 1) * 128] = emb_f[b * PD : (b + 1) * PD, :].astype(BF)

    @pl.loop(1, NZ)
    def _(k):
        zz = (z + k) % NZ
        remote(emb_s, emb_l.at[s], emb_ss.at[k], emb_rs.at[z], g, x * NZ + zz).start()

    send_rows(2)

    local_copies[2].wait()
    gather_rest(ww_v, ww_rs, fw_ss)

    @pl.loop(1, NZ)
    def _(k):
        zz = (z + k) % NZ
        wait_in(emb_l.at[x * NZ + zz], emb_rs.at[zz])

    line = emb_l.at[pl.ds(x * NZ, NZ)]

    @pl.loop(1, NX)
    def _(k):
        xx = (x + k) % NX
        remote(line, line, line_ss.at[k], line_rs.at[x], g, xx * NZ + z).start()

    send_rows(3)

    @pl.loop(0, TOK // 256)
    def _(i):
        at = pl.multiple_of(i * 256, 256)
        hidden = jnp.tanh(
            jnp.dot(x_v[pl.ds(at, 256), :], ww_v[...].reshape(D, D), preferred_element_type=F32)
        )
        d1_v[pl.ds(at, 256), :] = 1.0 - hidden * hidden
        q_at = pl.multiple_of(i * 8, 8)
        qv_f[pl.ds(q_at, 8), :] = jnp.sum(hidden.reshape(8, QL, D), axis=1) * (1.0 / QL)

    qv_v[...] = qv_f[...].astype(BF)

    def score(i):
        xx = (x + NX - i) % NX

        @pl.loop(0, NZ)
        def _(k):
            o = xx * NZ + (z + NZ + NZ - 1 - k) % NZ

            @pl.when(o != s)
            def _():
                wait_in(answer.at[o], row_rs.at[o])

        got = answer[pl.ds(xx * NZ, NZ)].reshape(NZ * CAP, D)
        s_v[:, pl.ds(pl.multiple_of(xx * NZ * CAP, NZ * CAP), NZ * CAP)] = lax.dot_general(
            qv_v[...], got, nt, preferred_element_type=F32
        )

    pl.loop(0, NX - 1)(score)

    @pl.loop(1, NX)
    def _(k):
        xx = (x + k) % NX
        wait_in(emb_l.at[pl.ds(xx * NZ, NZ)], line_rs.at[xx])

    pieces = emb_l[...].reshape(NS * 32, 128)
    to_passage, from_piece = iota((128, NS * 32), 0), iota((128, NS * 32), 1)
    for b in range(8):
        pick = (from_piece == (to_passage // PD) * 32 + b * PD + to_passage % PD)
        e_v[:, b * 128 : (b + 1) * 128] = jnp.dot(
            pick.astype(F32).astype(BF), pieces, preferred_element_type=F32
        ).astype(BF)

    in_logits = (
        lax.dot_general(qv_v[...], e_v[...], nt, preferred_element_type=F32) / logit_divisor
    )

    score(NX - 1)
    named = mask_v[...] > 0.5
    neg_logits = jnp.where(named, s_v[...] / logit_divisor, -jnp.inf)
    top = jnp.maximum(
        jnp.max(in_logits, axis=1, keepdims=True), jnp.max(neg_logits, axis=1, keepdims=True)
    )
    in_exp = jnp.exp(in_logits - top)
    neg_exp = jnp.where(named, jnp.exp(neg_logits - top), 0.0)
    total = jnp.sum(in_exp, axis=1, keepdims=True) + jnp.sum(neg_exp, axis=1, keepdims=True)
    label = (iota((QD, 128), 1) == to_column(pos_ref[...].astype(F32), QD).astype(jnp.int32))
    label = label.astype(F32)
    picked = jnp.sum(in_logits * label, axis=1, keepdims=True)
    loss_ref[...] = to_row(jnp.log(total) + top - picked, QD)
    coeff_in = (in_exp / total - label).astype(BF)
    coeff_neg = (neg_exp / total).astype(BF)
    query_grad = jnp.dot(coeff_in, e_v[...], preferred_element_type=F32) + jnp.dot(
        coeff_neg, answer[...].reshape(SLOTS, D), preferred_element_type=F32
    )
    qg_v[...] = query_grad * GRAD_SCALE * (1.0 / QL)

    @pl.loop(0, QD // 8)
    def _(i):
        q_at = pl.multiple_of(i * 8, 8)
        grads = qg_v[pl.ds(q_at, 8), :]
        for j in range(8):
            at = pl.multiple_of(i * 256 + j * QL, QL)
            value = (d1_v[pl.ds(at, QL), :] * grads[j : j + 1, :]).astype(BF)
            hg_v[0, pl.ds(at, QL), :] = value[:, : D // 2]
            hg_v[1, pl.ds(at, QL), :] = value[:, D // 2 :]

    def finish(i):
        xx = (x + 1 + i) % NX
        wait_in(ex_l.at[i], ex_rs.at[i])
        both = own_v[i % 2] + ex_l[i].astype(F32)
        part_a, part_b = both[:RA], both[RA:]
        acc_b[xx] = part_b
        b_s[xx] = part_b.astype(BF)
        for k in range(NY):
            piece = part_a[:, k * 128 : (k + 1) * 128]
            acc_a[k, xx] = piece
            a_s[k, xx] = piece.astype(BF)

        @pl.when(i < NX - 1)
        def _():
            remote(b_s.at[xx], b_l.at[i], b_ss.at[i], b_rs.at[i], g, xx * NZ + z).start()

        @pl.loop(1, NY)
        def _(k):
            yy = (y + k) % NY
            remote(
                a_s.at[yy, xx], a_l.at[k - 1, xx], a_ss.at[k - 1, i], a_rs.at[k - 1, i],
                yy * NC + c, s,
            ).start()

    @pl.loop(0, NX)
    def _(i):
        xx = (x + 1 + i) % NX
        left = xt_v[pl.ds(pl.multiple_of(xx * 256, 256), 256), :]
        ex_s[i] = jnp.dot(left, hg_v[1 - c], preferred_element_type=F32).astype(BF)
        remote(ex_s.at[i], ex_l.at[i], ex_ss.at[i], ex_rs.at[i], sib, s).start()

        @pl.when(i > 0)
        def _():
            finish(i - 1)

        own_v[i % 2] = jnp.dot(left, hg_v[c], preferred_element_type=F32)

    finish(NX - 1)

    @pl.loop(0, NX)
    def _(i):
        xx = (x + 1 + i) % NX
        part = acc_a[y, xx]
        for k in range(1, NY):
            wait_in(a_l.at[k - 1, xx], a_rs.at[k - 1, i])
            part = part + a_l[k - 1, xx].astype(F32)

        @pl.when(i < NX - 1)
        def _():
            a2_s[i] = part.astype(BF)
            remote(a2_s.at[i], a2_l.at[i], a2_ss.at[i], a2_rs.at[i], g, xx * NZ + z).start()

        @pl.when(i == NX - 1)
        def _():
            a2_o[...] = part

    part_b = acc_b[x]
    for k in range(NX - 1):
        wait_in(b_l.at[k], b_rs.at[k])
        part_b = part_b + b_l[k].astype(F32)
    for k in range(NY):
        piece = part_b[:, k * 128 : (k + 1) * 128]
        b2_o[k] = piece
        b2_s[k] = piece.astype(BF)

    @pl.loop(1, NY)
    def _(k):
        yy = (y + k) % NY
        remote(b2_s.at[yy], b2_l.at[k - 1], b2_ss.at[k - 1], b2_rs.at[k - 1], yy * NC + c, s).start()

    @pl.loop(1, NS)
    def _(k):
        o = (s + k) % NS
        wait_out(req_s.at[o], req_ss.at[o])
        wait_out(found.at[o], row_ss.at[o])

    @pl.loop(1, NZ)
    def _(k):
        wait_out(emb_s, emb_ss.at[k])

    @pl.loop(1, NX)
    def _(k):
        wait_out(emb_l.at[pl.ds(0, NZ)], line_ss.at[k])

    for buf, ss, fs in ((wp_v, wp_ss, fp_ss), (ww_v, ww_ss, fw_ss)):

        @pl.loop(0, NY)
        def _(k):
            wait_out(buf.at[g], ss.at[k])

        @pl.loop(1, NY)
        def _(k):
            wait_out(buf.at[((y + k) % NY) * NC + c], fs.at[k])

    part_a = a2_o[...]
    for k in range(NX - 1):
        wait_in(a2_l.at[k], a2_rs.at[k])
        part_a = part_a + a2_l[k].astype(F32)
    part_b = b2_o[y]
    for k in range(NY - 1):
        wait_in(b2_l.at[k], b2_rs.at[k])
        part_b = part_b + b2_l[k].astype(F32)
    part_a = part_a.reshape(RA // 32, 32, 128)
    part_b = part_b.reshape(RB // 32, 32, 128)
    z_o[: RA // 32] = part_a
    z_o[RA // 32 :] = part_b
    z_s[: RA // 32] = part_a.astype(BF)
    z_s[RA // 32 :] = part_b.astype(BF)

    @pl.loop(1, NZ)
    def _(k):
        zz = (z + k) % NZ
        remote(z_s.at[zz], z_l.at[k - 1], z_ss.at[k - 1], z_rs.at[k - 1], g, x * NZ + zz).start()

    @pl.loop(0, NX)
    def _(i):
        wait_out(ex_s.at[i], ex_ss.at[i])

        @pl.loop(0, NY - 1)
        def _(k):
            wait_out(a_s.at[0, 0], a_ss.at[k, i])

    @pl.loop(0, NX - 1)
    def _(i):
        wait_out(b_s.at[i], b_ss.at[i])
        wait_out(a2_s.at[i], a2_ss.at[i])

    @pl.loop(0, NY - 1)
    def _(i):
        wait_out(b2_s.at[i], b2_ss.at[i])

    total_part = z_o[z]
    for k in range(NZ - 1):
        wait_in(z_l.at[k], z_rs.at[k])
        total_part = total_part + z_l[k].astype(F32)

    f_s[...] = total_part.astype(BF)
    f_l[g] = total_part.astype(BF)

    @pl.loop(1, NG)
    def _(k):
        gg = (g + k) % NG
        remote(f_s, f_l.at[g], f_ss.at[k], f_rs.at[g], gg, s).start()

    @pl.loop(0, NZ - 1)
    def _(i):
        wait_out(z_s.at[i], z_ss.at[i])

    @pl.loop(1, NG)
    def _(k):
        gg = (g + k) % NG
        wait_in(f_l.at[gg], f_rs.at[gg])

    for yy in range(NY):
        for cc in range(NC):
            at = (cc * NY + yy) * 128
            grad_ref[:, at : at + 128] = f_l[yy * NC + cc].astype(F32)

    @pl.loop(1, NG)
    def _(k):
        wait_out(f_s, f_ss.at[k])


def hand_over(grad, loss, emb, grad_out, loss_out, emb_out):
    grad_out[...] = grad[...]
    loss_out[...] = loss[...]
    emb_out[...] = emb[...]


def shards(
    query_states, passage_states, index_rows, weight, prev_weight, neg_owner, neg_row, positive
):
    vmem = pl.BlockSpec(memory_space=pltpu.VMEM)
    hbm = pl.BlockSpec(memory_space=pltpu.HBM)
    dma = pltpu.SemaphoreType.DMA
    half = D // 2
    scratch = [
        pltpu.VMEM((NEG, 1, QD), jnp.int32),
        pltpu.VMEM((NEG, QD), jnp.int32),
        pltpu.VMEM((1, QD), jnp.int32),
        pltpu.VMEM((TOK, D), BF),
        pltpu.VMEM((D, TOK), BF),
        pltpu.VMEM((PD * PL, D), BF),
        pltpu.VMEM((ROWS, D), BF),
        pltpu.VMEM((NG, D // NG, D), BF),
        pltpu.VMEM((NG, D // NG, D), BF),
        pltpu.VMEM((NS, 1, 128), F32),
        pltpu.VMEM((NS, 1, 128), F32),
        pltpu.VMEM((NS, CAP, D), BF),
        pltpu.VMEM((NS, CAP, D), BF),
        pltpu.VMEM((QD, SLOTS), F32),
        pltpu.VMEM((32, 128), F32),
        pltpu.VMEM((32, 128), BF),
        pltpu.VMEM((NS, 32, 128), BF),
        pltpu.VMEM((NS * PD, D), BF),
        pltpu.VMEM((TOK, D), F32),
        pltpu.VMEM((QD, D), F32),
        pltpu.VMEM((QD, D), BF),
        pltpu.VMEM((QD, SLOTS), F32),
        pltpu.VMEM((QD, D), F32),
        pltpu.VMEM((2, TOK, half), BF),
        pltpu.VMEM((NX, 256, half), BF),
        pltpu.VMEM((NX, 256, half), BF),
        pltpu.VMEM((2, 256, half), F32),
        pltpu.VMEM((NY, NX, RA, 128), F32),
        pltpu.VMEM((NX, RB, half), F32),
        pltpu.VMEM((NY, NX, RA, 128), BF),
        pltpu.VMEM((NX, RB, half), BF),
        pltpu.VMEM((NY - 1, NX, RA, 128), BF),
        pltpu.VMEM((NX - 1, RB, half), BF),
        pltpu.VMEM((NX - 1, RA, 128), BF),
        pltpu.VMEM((NY, RB, 128), BF),
        pltpu.VMEM((NX - 1, RA, 128), BF),
        pltpu.VMEM((NY - 1, RB, 128), BF),
        pltpu.VMEM((RA, 128), F32),
        pltpu.VMEM((NY, RB, 128), F32),
        pltpu.VMEM((NZ, 32, 128), BF),
        pltpu.VMEM((NZ - 1, 32, 128), BF),
        pltpu.VMEM((NZ, 32, 128), F32),
        pltpu.VMEM((32, 128), BF),
        pltpu.VMEM((NG, 32, 128), BF),
        dma((8,)),
        dma((NS,)), dma((NS,)),
        dma((NS,)), dma((NS,)),
        dma((NY,)), dma((NG,)),
        dma((NY,)), dma((NG,)),
        dma((NY,)), dma((NY,)),
        dma((NZ,)), dma((NZ,)),
        dma((NX,)), dma((NX,)),
        dma((NX,)), dma((NX,)),
        dma((NY - 1, NX)), dma((NY - 1, NX)),
        dma((NX - 1,)), dma((NX - 1,)),
        dma((NX - 1,)), dma((NX - 1,)),
        dma((NY - 1,)), dma((NY - 1,)),
        dma((NZ - 1,)), dma((NZ - 1,)),
        dma((NG,)), dma((NG,)),
    ]
    grad, loss, emb = pl.pallas_call(
        kernel,
        out_shape=(
            jax.ShapeDtypeStruct((D // NS, D), F32),
            jax.ShapeDtypeStruct((1, QD), F32),
            jax.ShapeDtypeStruct((PD, D), BF),
        ),
        in_specs=[hbm] * 8,
        out_specs=(vmem, vmem, vmem),
        scratch_shapes=scratch,
        compiler_params=pltpu.CompilerParams(
            collective_id=0, has_side_effects=True, vmem_limit_bytes=60 << 20
        ),
        cost_estimate=pl.CostEstimate(
            flops=16 * 2**30, bytes_accessed=12 * 2**20, transcendentals=3 * 2**20
        ),
        name="retriever_step",
    )(
        neg_owner.transpose(1, 2, 0),
        neg_row.T,
        positive.reshape(1, QD),
        query_states.reshape(TOK, D),
        passage_states.reshape(PD * PL, D),
        index_rows,
        weight,
        prev_weight,
    )
    grad, loss, emb = pl.pallas_call(
        hand_over,
        out_shape=(
            jax.ShapeDtypeStruct((D // NS, D), F32),
            jax.ShapeDtypeStruct((1, QD), F32),
            jax.ShapeDtypeStruct((PD, D), BF),
        ),
        in_specs=[vmem] * 3,
        out_specs=(vmem, vmem, vmem),
        name="hand_over",
    )(grad, loss, emb)
    return grad, loss.reshape(QD), emb


def solution(mesh):
    return jax.shard_map(
        shards,
        mesh=mesh,
        in_specs=(
            P(("group", "shard"), None, None),
            P(("group", "shard"), None, None),
            P(("group", "shard"), None),
            P("group", None),
            P("group", None),
            P(("group", "shard"), None, None),
            P(("group", "shard"), None),
            P(("group", "shard")),
        ),
        out_specs=(P("shard", None), P(("group", "shard")), P(("group", "shard"), None)),
        check_vma=False,
    )
```

```python
import functools
import math

import jax
import jax.numpy as jnp
from jax import lax
from jax.experimental import pallas as pl
from jax.experimental.pallas import tpu as pltpu
from jax.sharding import PartitionSpec as P

MESH = pl.DeviceIdType.MESH
BF = jnp.bfloat16
F32 = jnp.float32

logit_divisor = 0.05

D = 1024
QD = 64
QL = 32
PD = 4
PL = 128
NEG = 8
ROWS = 2048
CAP = 32
NY, NC, NX, NZ = 4, 2, 4, 8
NG, NS = NY * NC, NX * NZ
TOK = QD * QL
SLOTS = NS * CAP
ZA, ZB = 5, 3
RA, RB = ZA * 32, ZB * 32
GRAD_SCALE = 1.0 / (logit_divisor * math.sqrt(QD * NS * NG))


def iota(shape, axis):
    return lax.broadcasted_iota(jnp.int32, shape, axis)


def to_column(row, n):
    eye = iota((n, n), 0) == iota((n, n), 1)
    return jnp.sum(jnp.where(eye, row, jnp.zeros_like(row)), axis=1, keepdims=True)


def to_row(column, n):
    eye = iota((n, n), 0) == iota((n, n), 1)
    return jnp.sum(jnp.where(eye, column, jnp.zeros_like(column)), axis=0, keepdims=True)


def kernel(
    owner_hbm, row_hbm, pos_hbm, x_hbm, p_hbm, idx_hbm, w_hbm, pw_hbm,
    grad_ref, loss_ref, emb_ref,
    owner_ref, row_ref, pos_ref, x_v, xt_v, p_v, idx_v, wp_v, ww_v,
    req_s, req_l, found, answer, mask_v,
    emb_f, emb_s, emb_l, e_v,
    d1_v, qv_f, qv_v, s_v, qg_v, hg_v,
    ex_s, ex_l, own_v, acc_a, acc_b, a_s, b_s, a_l, b_l,
    za_s, zb_s, za_o, zb_o, z_l, f_s, f_l,
    loc_sem, req_ss, req_rs, row_ss, row_rs, wp_ss, wp_rs, ww_ss, ww_rs,
    fp_ss, fw_ss, emb_ss, emb_rs, line_ss, line_rs, ex_ss, ex_rs, a_ss, a_rs, b_ss, b_rs,
    za_ss, zb_ss, z_rs, f_ss, f_rs,
):
    g, s = lax.axis_index("group"), lax.axis_index("shard")
    y, c = g // NC, g % NC
    x, z = s // NZ, s % NZ
    sib = y * NC + 1 - c

    def local(src, dst, k):
        return pltpu.make_async_copy(src, dst, loc_sem.at[k])

    def remote(src, dst, ss, rs, gg, sh):
        return pltpu.make_async_remote_copy(
            src_ref=src, dst_ref=dst, send_sem=ss, recv_sem=rs,
            device_id=(gg, sh), device_id_type=MESH,
        )

    def wait_in(dst, rs):
        remote(dst, dst, rs, rs, sib, s).wait_recv()

    def wait_out(src, ss):
        remote(src, src, ss, ss, sib, s).wait_send()

    nt = (((1,), (1,)), ((), ()))

    small_copies = [
        local(owner_hbm, owner_ref, 5),
        local(row_hbm, row_ref, 6),
        local(pos_hbm, pos_ref, 7),
    ]
    for copy in small_copies:
        copy.start()

    barrier = pltpu.get_barrier_semaphore()

    @pl.loop(1, NS)
    def _(k):
        pl.semaphore_signal(barrier, inc=1, device_id=(g, (s + k) % NS), device_id_type=MESH)

    @pl.loop(1, NG)
    def _(k):
        pl.semaphore_signal(barrier, inc=1, device_id=((g + k) % NG, s), device_id_type=MESH)

    @pl.loop(1, NY)
    def _(k):
        @pl.loop(1, NZ)
        def _(j):
            peer = ((y + k) % NY * NC + c, x * NZ + (z + j) % NZ)
            pl.semaphore_signal(barrier, inc=1, device_id=peer, device_id_type=MESH)

    local_copies = [
        local(idx_hbm, idx_v, 0),
        local(pw_hbm, wp_v.at[g], 1),
        local(w_hbm, ww_v.at[g], 2),
        local(x_hbm, x_v, 3),
        local(p_hbm, p_v, 4),
    ]
    for copy in local_copies:
        copy.start()

    for copy in small_copies:
        copy.wait()
    upper = (iota((QD, QD), 0) < iota((QD, QD), 1)).astype(F32).astype(BF)
    base = jnp.zeros((NS, 1), F32)
    requests = jnp.zeros((NS, 128), F32)
    slots = []
    for n in range(NEG):
        owner = owner_ref[n]
        hot = (iota((NS, QD), 0) == owner).astype(F32)
        hot_bf = hot.astype(BF)
        before = jnp.dot(hot_bf, upper, preferred_element_type=F32) + base
        rank = jnp.sum(hot * before, axis=0, keepdims=True).astype(jnp.int32)
        base = base + jnp.sum(hot, axis=1, keepdims=True)
        slots.append((owner * CAP + rank).astype(F32))
        row = row_ref[n : n + 1, :]
        here = iota((128, QD), 0) == rank + (s % 4) * CAP
        high = jnp.where(here, row // 16, 0).astype(F32).astype(BF)
        low = jnp.where(here, row % 16, 0).astype(F32).astype(BF)
        requests = requests + (
            16.0 * lax.dot_general(hot_bf, high, nt, preferred_element_type=F32)
            + lax.dot_general(hot_bf, low, nt, preferred_element_type=F32)
        )
    for o in range(NS):
        req_s[o] = requests[o : o + 1, :]

    pl.semaphore_wait(barrier, NS - 1 + NG - 1 + (NY - 1) * (NZ - 1))

    @pl.loop(1, NS)
    def _(k):
        o = (x + k // NZ) % NX * NZ + (z + k) % NZ
        remote(req_s.at[o], req_l.at[s], req_ss.at[o], req_rs.at[s], g, o).start()

    req_l[s] = req_s[s]

    for hbm, buf, ss, rs in ((pw_hbm, wp_v, wp_ss, wp_rs), (w_hbm, ww_v, ww_ss, ww_rs)):

        @pl.loop(1, NY)
        def _(k):
            peer = ((y + k) % NY) * NC + c
            remote(hbm, buf.at[g], ss.at[k], rs.at[g], peer, s).start()

        remote(hbm, buf.at[g], ss.at[0], rs.at[g], sib, s).start()

    local_copies[0].wait()
    row_lane = iota((128, ROWS), 1)

    sets = ((4, 1, 2, 7), (0, 5, 6, 3))

    def send_rows(i, half):
        for step in sets[half]:
            r = (x + i) % NX * NZ + (z + step) % NZ

            def send():
                remote(
                    found.at[i, half, r % 4], answer.at[s], row_ss.at[r], row_rs.at[s], g, r
                ).start()

            if step:
                send()
            else:
                pl.when(i > 0)(send)

    @pl.loop(0, NX)
    def _(i):
        for half in range(2):
            ids = jnp.zeros((1, 128), F32)
            for step in sets[half]:
                r = (x + i) % NX * NZ + (z + step) % NZ

                def wait():
                    wait_in(req_l.at[r], req_rs.at[r])

                if step:
                    wait()
                else:
                    pl.when(i > 0)(wait)
                ids = ids + req_l[r]
            column = to_column(ids, 128).astype(jnp.int32)
            hot = (row_lane == column).astype(F32).astype(BF)
            got = jnp.dot(hot, idx_v[...], preferred_element_type=F32).astype(BF)
            found[i, half] = got.reshape(4, CAP, D)

            @pl.when(i < NX // 2)
            def _():
                send_rows(i, half)

    answer[s] = found[0, 1, s % 4]

    slot_lane = iota((QD, SLOTS), 1)
    mask = jnp.zeros((QD, SLOTS), F32)
    for n in range(NEG):
        mask = mask + (slot_lane == to_column(slots[n], QD).astype(jnp.int32)).astype(F32)
    mask_v[...] = mask

    local_copies[3].wait()

    @pl.loop(0, TOK // 256)
    def _(i):
        at = pl.multiple_of(i * 256, 256)
        xt_v[:, pl.ds(at, 256)] = x_v[pl.ds(at, 256), :].T

    def gather_rest(buf, rs, fs):
        @pl.loop(1, NY)
        def _(k):
            peer = ((y + k) % NY) * NC + c
            wait_in(buf.at[peer], rs.at[peer])
            remote(buf.at[peer], buf.at[peer], fs.at[k], rs.at[peer], sib, s).start()

        @pl.loop(0, NY)
        def _(k):
            peer = k * NC + 1 - c
            wait_in(buf.at[peer], rs.at[peer])

    local_copies[1].wait()
    local_copies[4].wait()
    gather_rest(wp_v, wp_rs, fp_ss)
    for i in range(PD // 2):
        hidden = jnp.tanh(
            jnp.dot(
                p_v[i * 2 * PL : (i + 1) * 2 * PL, :],
                wp_v[...].reshape(D, D),
                preferred_element_type=F32,
            )
        )
        for j in range(2):
            mean = jnp.sum(hidden[j * PL : (j + 1) * PL], axis=0, keepdims=True) * (1.0 / PL)
            p = i * 2 + j
            for b in range(8):
                emb_f[b * PD + p : b * PD + p + 1, :] = mean[:, b * 128 : (b + 1) * 128]
    emb = emb_f[...].astype(BF)
    emb_s[...] = emb
    emb_l[s] = emb
    for b in range(8):
        emb_ref[:, b * 128 : (b + 1) * 128] = emb_f[b * PD : (b + 1) * PD, :].astype(BF)

    @pl.loop(1, NZ)
    def _(k):
        zz = (z + k) % NZ
        remote(emb_s, emb_l.at[s], emb_ss.at[k], emb_rs.at[z], g, x * NZ + zz).start()

    send_rows(2, 0)
    send_rows(2, 1)

    local_copies[2].wait()
    gather_rest(ww_v, ww_rs, fw_ss)

    @pl.loop(1, NZ)
    def _(k):
        zz = (z + k) % NZ
        wait_in(emb_l.at[x * NZ + zz], emb_rs.at[zz])

    line = emb_l.at[pl.ds(x * NZ, NZ)]

    @pl.loop(1, NX)
    def _(k):
        xx = (x + k) % NX
        remote(line, line, line_ss.at[k], line_rs.at[x], g, xx * NZ + z).start()

    send_rows(3, 0)
    send_rows(3, 1)

    @pl.loop(0, TOK // 256)
    def _(i):
        at = pl.multiple_of(i * 256, 256)
        hidden = jnp.tanh(
            jnp.dot(x_v[pl.ds(at, 256), :], ww_v[...].reshape(D, D), preferred_element_type=F32)
        )
        d1_v[pl.ds(at, 256), :] = 1.0 - hidden * hidden
        q_at = pl.multiple_of(i * 8, 8)
        qv_f[pl.ds(q_at, 8), :] = jnp.sum(hidden.reshape(8, QL, D), axis=1) * (1.0 / QL)

    qv_v[...] = qv_f[...].astype(BF)

    def score(i):
        xx = (x + NX - i) % NX

        @pl.loop(0, NZ)
        def _(k):
            o = xx * NZ + (z + NZ + NZ - 1 - k) % NZ

            @pl.when(o != s)
            def _():
                wait_in(answer.at[o], row_rs.at[o])

        got = answer[pl.ds(xx * NZ, NZ)].reshape(NZ * CAP, D)
        s_v[:, pl.ds(pl.multiple_of(xx * NZ * CAP, NZ * CAP), NZ * CAP)] = lax.dot_general(
            qv_v[...], got, nt, preferred_element_type=F32
        )

    pl.loop(0, NX - 1)(score)

    @pl.loop(1, NX)
    def _(k):
        xx = (x + k) % NX
        wait_in(emb_l.at[pl.ds(xx * NZ, NZ)], line_rs.at[xx])

    pieces = emb_l[...].reshape(NS * 32, 128)
    to_passage, from_piece = iota((128, NS * 32), 0), iota((128, NS * 32), 1)
    for b in range(8):
        pick = (from_piece == (to_passage // PD) * 32 + b * PD + to_passage % PD)
        e_v[:, b * 128 : (b + 1) * 128] = jnp.dot(
            pick.astype(F32).astype(BF), pieces, preferred_element_type=F32
        ).astype(BF)

    in_logits = (
        lax.dot_general(qv_v[...], e_v[...], nt, preferred_element_type=F32) / logit_divisor
    )

    score(NX - 1)
    named = mask_v[...] > 0.5
    neg_logits = jnp.where(named, s_v[...] / logit_divisor, -jnp.inf)
    top = jnp.maximum(
        jnp.max(in_logits, axis=1, keepdims=True), jnp.max(neg_logits, axis=1, keepdims=True)
    )
    in_exp = jnp.exp(in_logits - top)
    neg_exp = jnp.where(named, jnp.exp(neg_logits - top), 0.0)
    total = jnp.sum(in_exp, axis=1, keepdims=True) + jnp.sum(neg_exp, axis=1, keepdims=True)
    label = (iota((QD, 128), 1) == to_column(pos_ref[...].astype(F32), QD).astype(jnp.int32))
    label = label.astype(F32)
    picked = jnp.sum(in_logits * label, axis=1, keepdims=True)
    loss_ref[...] = to_row(jnp.log(total) + top - picked, QD)
    coeff_in = (in_exp / total - label).astype(BF)
    coeff_neg = (neg_exp / total).astype(BF)
    query_grad = jnp.dot(coeff_in, e_v[...], preferred_element_type=F32) + jnp.dot(
        coeff_neg, answer[...].reshape(SLOTS, D), preferred_element_type=F32
    )
    qg_v[...] = query_grad * GRAD_SCALE * (1.0 / QL)

    @pl.loop(0, QD // 8)
    def _(i):
        q_at = pl.multiple_of(i * 8, 8)
        grads = qg_v[pl.ds(q_at, 8), :]
        for j in range(8):
            at = pl.multiple_of(i * 256 + j * QL, QL)
            value = (d1_v[pl.ds(at, QL), :] * grads[j : j + 1, :]).astype(BF)
            hg_v[0, pl.ds(at, QL), :] = value[:, : D // 2]
            hg_v[1, pl.ds(at, QL), :] = value[:, D // 2 :]

    def finish(i):
        xx = (x + 1 + i) % NX
        wait_in(ex_l.at[i], ex_rs.at[i])
        both = own_v[i % 2] + ex_l[i].astype(F32)
        part_a, part_b = both[:RA], both[RA:]
        acc_b[xx] = part_b
        b_s[xx] = part_b.astype(BF)
        for k in range(NY):
            piece = part_a[:, k * 128 : (k + 1) * 128]
            acc_a[k, xx] = piece
            a_s[k, xx] = piece.astype(BF)

        @pl.when(i < NX - 1)
        def _():
            remote(b_s.at[xx], b_l.at[i], b_ss.at[i], b_rs.at[i], g, xx * NZ + z).start()

        @pl.loop(1, NY)
        def _(k):
            yy = (y + k) % NY
            remote(
                a_s.at[yy, xx], a_l.at[k - 1, xx], a_ss.at[k - 1, i], a_rs.at[k - 1, i],
                yy * NC + c, s,
            ).start()

    @pl.loop(0, NX)
    def _(i):
        xx = (x + 1 + i) % NX
        left = xt_v[pl.ds(pl.multiple_of(xx * 256, 256), 256), :]
        ex_s[i] = jnp.dot(left, hg_v[1 - c], preferred_element_type=F32).astype(BF)
        remote(ex_s.at[i], ex_l.at[i], ex_ss.at[i], ex_rs.at[i], sib, s).start()

        @pl.when(i > 0)
        def _():
            finish(i - 1)

        own_v[i % 2] = jnp.dot(left, hg_v[c], preferred_element_type=F32)

    finish(NX - 1)

    def second_a(i):
        xx = (x + 1 + i) % NX
        part = acc_a[y, xx]
        for k in range(1, NY):
            wait_in(a_l.at[k - 1, xx], a_rs.at[k - 1, i])
            part = part + a_l[k - 1, xx].astype(F32)
        part = part.reshape(ZA, 32, 128)
        za_s[xx] = part.astype(BF)

        @pl.when(i == NX - 1)
        def _():
            za_o[...] = part

        @pl.loop(0, NZ)
        def _(k):
            zz = (z + 1 + k) % NZ

            @pl.when(zz < ZA)
            def _():
                @pl.when(xx * NZ + zz != s)
                def _():
                    remote(
                        za_s.at[xx, zz], z_l.at[s], za_ss.at[xx, zz], z_rs.at[s], g, xx * NZ + zz
                    ).start()

    pl.loop(0, NX - 1)(second_a)

    part_b = acc_b[x]
    for k in range(NX - 1):
        wait_in(b_l.at[k], b_rs.at[k])
        part_b = part_b + b_l[k].astype(F32)
    for k in range(NY):
        piece = part_b[:, k * 128 : (k + 1) * 128].reshape(ZB, 32, 128)
        zb_o[k] = piece
        zb_s[k] = piece.astype(BF)

    @pl.loop(0, NY)
    def _(k):
        yy = (y + 1 + k) % NY

        @pl.loop(0, ZB)
        def _(j):
            @pl.when((yy - y) * NZ + ZA + j - z != 0)
            def _():
                remote(
                    zb_s.at[yy, j], z_l.at[y * NZ + z], zb_ss.at[yy, j], z_rs.at[y * NZ + z],
                    yy * NC + c, x * NZ + ZA + j,
                ).start()

    second_a(NX - 1)

    @pl.loop(1, NS)
    def _(k):
        o = (s + k) % NS
        wait_out(req_s.at[o], req_ss.at[o])
        wait_out(found.at[0, 0, 0], row_ss.at[o])

    @pl.loop(1, NZ)
    def _(k):
        wait_out(emb_s, emb_ss.at[k])

    @pl.loop(1, NX)
    def _(k):
        wait_out(emb_l.at[pl.ds(0, NZ)], line_ss.at[k])

    for buf, ss, fs in ((wp_v, wp_ss, fp_ss), (ww_v, ww_ss, fw_ss)):

        @pl.loop(0, NY)
        def _(k):
            wait_out(buf.at[g], ss.at[k])

        @pl.loop(1, NY)
        def _(k):
            wait_out(buf.at[((y + k) % NY) * NC + c], fs.at[k])

    @pl.loop(0, NX)
    def _(i):
        wait_out(ex_s.at[i], ex_ss.at[i])

        @pl.loop(0, NY - 1)
        def _(k):
            wait_out(a_s.at[0, 0], a_ss.at[k, i])

    @pl.loop(0, NX - 1)
    def _(i):
        wait_out(b_s.at[i], b_ss.at[i])

    def collect(me, own):
        @pl.loop(1, NS)
        def _(k):
            wait_in(z_l.at[(me + k) % NS], z_rs.at[(me + k) % NS])

        total_part = own
        for k in range(1, NS):
            total_part = total_part + z_l[(me + k) % NS].astype(F32)
        f_s[...] = total_part.astype(BF)

    @pl.when(z < ZA)
    def _():
        collect(x * NZ + z, za_o[z])

    @pl.when(z >= ZA)
    def _():
        collect(y * NZ + z, zb_o[y, z - ZA])

    f_l[g] = f_s[...]

    @pl.loop(1, NG)
    def _(k):
        gg = (g + k) % NG
        remote(f_s, f_l.at[g], f_ss.at[k], f_rs.at[g], gg, s).start()

    @pl.loop(0, NX)
    def _(i):
        @pl.loop(0, ZA)
        def _(k):
            @pl.when((i - x) * NZ + k - z != 0)
            def _():
                wait_out(za_s.at[i, k], za_ss.at[i, k])

        @pl.loop(0, ZB)
        def _(k):
            @pl.when((i - y) * NZ + ZA + k - z != 0)
            def _():
                wait_out(zb_s.at[i, k], zb_ss.at[i, k])

    @pl.loop(1, NG)
    def _(k):
        gg = (g + k) % NG
        wait_in(f_l.at[gg], f_rs.at[gg])

    grad_ref[...] = f_l[...]

    @pl.loop(1, NG)
    def _(k):
        wait_out(f_s, f_ss.at[k])


def hand_over(grad, loss, emb, grad_out, loss_out, emb_out):
    for y in range(NY):
        for c in range(NC):
            at = (c * NY + y) * 128
            grad_out[:, at : at + 128] = grad[y * NC + c].astype(F32)
    loss_out[...] = loss[...]
    emb_out[...] = emb[...]


def shards(
    query_states, passage_states, index_rows, weight, prev_weight, neg_owner, neg_row, positive
):
    vmem = pl.BlockSpec(memory_space=pltpu.VMEM)
    hbm = pl.BlockSpec(memory_space=pltpu.HBM)
    dma = pltpu.SemaphoreType.DMA
    half = D // 2
    scratch = [
        pltpu.VMEM((NEG, 1, QD), jnp.int32),
        pltpu.VMEM((NEG, QD), jnp.int32),
        pltpu.VMEM((1, QD), jnp.int32),
        pltpu.VMEM((TOK, D), BF),
        pltpu.VMEM((D, TOK), BF),
        pltpu.VMEM((PD * PL, D), BF),
        pltpu.VMEM((ROWS, D), BF),
        pltpu.VMEM((NG, D // NG, D), BF),
        pltpu.VMEM((NG, D // NG, D), BF),
        pltpu.VMEM((NS, 1, 128), F32),
        pltpu.VMEM((NS, 1, 128), F32),
        pltpu.VMEM((NX, 2, 4, CAP, D), BF),
        pltpu.VMEM((NS, CAP, D), BF),
        pltpu.VMEM((QD, SLOTS), F32),
        pltpu.VMEM((32, 128), F32),
        pltpu.VMEM((32, 128), BF),
        pltpu.VMEM((NS, 32, 128), BF),
        pltpu.VMEM((NS * PD, D), BF),
        pltpu.VMEM((TOK, D), F32),
        pltpu.VMEM((QD, D), F32),
        pltpu.VMEM((QD, D), BF),
        pltpu.VMEM((QD, SLOTS), F32),
        pltpu.VMEM((QD, D), F32),
        pltpu.VMEM((2, TOK, half), BF),
        pltpu.VMEM((NX, 256, half), BF),
        pltpu.VMEM((NX, 256, half), BF),
        pltpu.VMEM((2, 256, half), F32),
        pltpu.VMEM((NY, NX, RA, 128), F32),
        pltpu.VMEM((NX, RB, half), F32),
        pltpu.VMEM((NY, NX, RA, 128), BF),
        pltpu.VMEM((NX, RB, half), BF),
        pltpu.VMEM((NY - 1, NX, RA, 128), BF),
        pltpu.VMEM((NX - 1, RB, half), BF),
        pltpu.VMEM((NX, ZA, 32, 128), BF),
        pltpu.VMEM((NY, ZB, 32, 128), BF),
        pltpu.VMEM((ZA, 32, 128), F32),
        pltpu.VMEM((NY, ZB, 32, 128), F32),
        pltpu.VMEM((NS, 32, 128), BF),
        pltpu.VMEM((32, 128), BF),
        pltpu.VMEM((NG, 32, 128), BF),
        dma((8,)),
        dma((NS,)), dma((NS,)),
        dma((NS,)), dma((NS,)),
        dma((NY,)), dma((NG,)),
        dma((NY,)), dma((NG,)),
        dma((NY,)), dma((NY,)),
        dma((NZ,)), dma((NZ,)),
        dma((NX,)), dma((NX,)),
        dma((NX,)), dma((NX,)),
        dma((NY - 1, NX)), dma((NY - 1, NX)),
        dma((NX - 1,)), dma((NX - 1,)),
        dma((NX, ZA)), dma((NY, ZB)), dma((NS,)),
        dma((NG,)), dma((NG,)),
    ]
    grad, loss, emb = pl.pallas_call(
        kernel,
        out_shape=(
            jax.ShapeDtypeStruct((NG, 32, 128), BF),
            jax.ShapeDtypeStruct((1, QD), F32),
            jax.ShapeDtypeStruct((PD, D), BF),
        ),
        in_specs=[hbm] * 8,
        out_specs=(vmem, vmem, vmem),
        scratch_shapes=scratch,
        compiler_params=pltpu.CompilerParams(
            collective_id=0, has_side_effects=True, vmem_limit_bytes=60 << 20
        ),
        cost_estimate=pl.CostEstimate(
            flops=16 * 2**30, bytes_accessed=12 * 2**20, transcendentals=3 * 2**20
        ),
        name="retriever_step",
    )(
        neg_owner.transpose(1, 2, 0),
        neg_row.T,
        positive.reshape(1, QD),
        query_states.reshape(TOK, D),
        passage_states.reshape(PD * PL, D),
        index_rows,
        weight,
        prev_weight,
    )
    grad, loss, emb = pl.pallas_call(
        hand_over,
        out_shape=(
            jax.ShapeDtypeStruct((D // NS, D), F32),
            jax.ShapeDtypeStruct((1, QD), F32),
            jax.ShapeDtypeStruct((PD, D), BF),
        ),
        in_specs=[vmem] * 3,
        out_specs=(vmem, vmem, vmem),
        name="hand_over",
    )(grad, loss, emb)
    return grad, loss.reshape(QD), emb


def solution(mesh):
    return jax.shard_map(
        shards,
        mesh=mesh,
        in_specs=(
            P(("group", "shard"), None, None),
            P(("group", "shard"), None, None),
            P(("group", "shard"), None),
            P("group", None),
            P("group", None),
            P(("group", "shard"), None, None),
            P(("group", "shard"), None),
            P(("group", "shard")),
        ),
        out_specs=(P("shard", None), P(("group", "shard")), P(("group", "shard"), None)),
        check_vma=False,
    )
```

```python
import functools
import math

import jax
import jax.numpy as jnp
from jax import lax
from jax.experimental import pallas as pl
from jax.experimental.pallas import tpu as pltpu
from jax.sharding import PartitionSpec as P

MESH = pl.DeviceIdType.MESH
BF = jnp.bfloat16
F32 = jnp.float32

logit_divisor = 0.05

D = 1024
QD = 64
QL = 32
PD = 4
PL = 128
NEG = 8
ROWS = 2048
CAP = 32
NY, NC, NX, NZ = 4, 2, 4, 8
NG, NS = NY * NC, NX * NZ
TOK = QD * QL
SLOTS = NS * CAP
ZA, ZB = 4, 4
RA, RB = ZA * 32, ZB * 32
GRAD_SCALE = 1.0 / (logit_divisor * math.sqrt(QD * NS * NG))


def iota(shape, axis):
    return lax.broadcasted_iota(jnp.int32, shape, axis)


def to_column(row, n):
    eye = iota((n, n), 0) == iota((n, n), 1)
    return jnp.sum(jnp.where(eye, row, jnp.zeros_like(row)), axis=1, keepdims=True)


def to_row(column, n):
    eye = iota((n, n), 0) == iota((n, n), 1)
    return jnp.sum(jnp.where(eye, column, jnp.zeros_like(column)), axis=0, keepdims=True)


def kernel(
    owner_hbm, row_hbm, pos_hbm, x_hbm, p_hbm, idx_hbm, w_hbm, pw_hbm,
    grad_hbm, loss_hbm, emb_hbm,
    owner_ref, row_ref, pos_ref, loss_v, x_v, xt_v, p_v, idx_v, wp_v, ww_v,
    req_s, req_l, found, answer, mask_v,
    emb_f, emb_s, emb_l, e_v,
    d1_v, qv_f, qv_v, s_v, qg_v, hg_v,
    ex_s, ex_l, own_v, acc_a, acc_b, a_s, b_s, a_l, b_l,
    za_s, zb_s, za_o, zb_o, z_l, f_s, f_l,
    loc_sem, req_ss, req_rs, row_ss, row_rs, wp_ss, wp_rs, ww_ss, ww_rs,
    fp_ss, fw_ss, emb_ss, emb_rs, line_ss, line_rs, ex_ss, ex_rs, a_ss, a_rs, b_ss, b_rs,
    za_ss, zb_ss, z_rs, f_ss, f_rs,
):
    g, s = lax.axis_index("group"), lax.axis_index("shard")
    y, c = g // NC, g % NC
    x, z = s // NZ, s % NZ
    sib = y * NC + 1 - c

    def local(src, dst, k):
        return pltpu.make_async_copy(src, dst, loc_sem.at[k])

    def remote(src, dst, ss, rs, gg, sh):
        return pltpu.make_async_remote_copy(
            src_ref=src, dst_ref=dst, send_sem=ss, recv_sem=rs,
            device_id=(gg, sh), device_id_type=MESH,
        )

    def wait_in(dst, rs):
        remote(dst, dst, rs, rs, sib, s).wait_recv()

    def wait_out(src, ss):
        remote(src, src, ss, ss, sib, s).wait_send()

    nt = (((1,), (1,)), ((), ()))

    small_copies = [
        local(owner_hbm, owner_ref, 5),
        local(row_hbm, row_ref, 6),
        local(pos_hbm, pos_ref, 7),
    ]
    for copy in small_copies:
        copy.start()

    barrier = pltpu.get_barrier_semaphore()

    @pl.loop(1, NS)
    def _(k):
        pl.semaphore_signal(barrier, inc=1, device_id=(g, (s + k) % NS), device_id_type=MESH)

    @pl.loop(1, NG)
    def _(k):
        pl.semaphore_signal(barrier, inc=1, device_id=((g + k) % NG, s), device_id_type=MESH)

    @pl.loop(1, NY)
    def _(k):
        @pl.loop(1, NZ)
        def _(j):
            peer = ((y + k) % NY * NC + c, x * NZ + (z + j) % NZ)
            pl.semaphore_signal(barrier, inc=1, device_id=peer, device_id_type=MESH)

    local_copies = [
        local(idx_hbm, idx_v, 0),
        local(pw_hbm, wp_v.at[g], 1),
        local(w_hbm, ww_v.at[g], 2),
        local(x_hbm, x_v, 3),
        local(p_hbm, p_v, 4),
    ]
    for copy in local_copies:
        copy.start()

    for copy in small_copies:
        copy.wait()
    upper = (iota((QD, QD), 0) < iota((QD, QD), 1)).astype(F32).astype(BF)
    base = jnp.zeros((NS, 1), F32)
    requests = jnp.zeros((NS, 128), F32)
    slots = []
    for n in range(NEG):
        owner = owner_ref[n]
        hot = (iota((NS, QD), 0) == owner).astype(F32)
        hot_bf = hot.astype(BF)
        before = jnp.dot(hot_bf, upper, preferred_element_type=F32) + base
        rank = jnp.sum(hot * before, axis=0, keepdims=True).astype(jnp.int32)
        base = base + jnp.sum(hot, axis=1, keepdims=True)
        slots.append((owner * CAP + rank).astype(F32))
        row = row_ref[n : n + 1, :]
        here = iota((128, QD), 0) == rank + (s % 4) * CAP
        high = jnp.where(here, row // 16, 0).astype(F32).astype(BF)
        low = jnp.where(here, row % 16, 0).astype(F32).astype(BF)
        requests = requests + (
            16.0 * lax.dot_general(hot_bf, high, nt, preferred_element_type=F32)
            + lax.dot_general(hot_bf, low, nt, preferred_element_type=F32)
        )
    for o in range(NS):
        req_s[o] = requests[o : o + 1, :]

    pl.semaphore_wait(barrier, NS - 1 + NG - 1 + (NY - 1) * (NZ - 1))

    @pl.loop(1, NS)
    def _(k):
        o = (x + k // NZ) % NX * NZ + (z + k) % NZ
        remote(req_s.at[o], req_l.at[s], req_ss.at[o], req_rs.at[s], g, o).start()

    req_l[s] = req_s[s]

    def spread(hbm, buf, ss, rs):

        @pl.loop(1, NY)
        def _(k):
            peer = ((y + k) % NY) * NC + c
            remote(hbm, buf.at[g], ss.at[k], rs.at[g], peer, s).start()

        remote(hbm, buf.at[g], ss.at[0], rs.at[g], sib, s).start()

    spread(pw_hbm, wp_v, wp_ss, wp_rs)

    local_copies[0].wait()
    row_lane = iota((128, ROWS), 1)

    sets = ((4, 1, 2, 7), (0, 5, 6, 3))

    def send_rows(i, half):
        for step in sets[half]:
            r = (x + i) % NX * NZ + (z + step) % NZ

            def send():
                remote(
                    found.at[i, half, r % 4], answer.at[s], row_ss.at[r], row_rs.at[s], g, r
                ).start()

            if step:
                send()
            else:
                pl.when(i > 0)(send)

    @pl.loop(0, NX)
    def _(i):
        for half in range(2):
            ids = jnp.zeros((1, 128), F32)
            for step in sets[half]:
                r = (x + i) % NX * NZ + (z + step) % NZ

                def wait():
                    wait_in(req_l.at[r], req_rs.at[r])

                if step:
                    wait()
                else:
                    pl.when(i > 0)(wait)
                ids = ids + req_l[r]
            column = to_column(ids, 128).astype(jnp.int32)
            hot = (row_lane == column).astype(F32).astype(BF)
            got = jnp.dot(hot, idx_v[...], preferred_element_type=F32).astype(BF)
            found[i, half] = got.reshape(4, CAP, D)

            @pl.when(i < NX // 2)
            def _():
                send_rows(i, half)

    answer[s] = found[0, 1, s % 4]
    spread(w_hbm, ww_v, ww_ss, ww_rs)

    slot_lane = iota((QD, SLOTS), 1)
    mask = jnp.zeros((QD, SLOTS), F32)
    for n in range(NEG):
        mask = mask + (slot_lane == to_column(slots[n], QD).astype(jnp.int32)).astype(F32)
    mask_v[...] = mask

    local_copies[3].wait()

    @pl.loop(0, TOK // 256)
    def _(i):
        at = pl.multiple_of(i * 256, 256)
        xt_v[:, pl.ds(at, 256)] = x_v[pl.ds(at, 256), :].T

    def gather_rest(buf, rs, fs):
        @pl.loop(1, NY)
        def _(k):
            peer = ((y + k) % NY) * NC + c
            wait_in(buf.at[peer], rs.at[peer])
            remote(buf.at[peer], buf.at[peer], fs.at[k], rs.at[peer], sib, s).start()

        @pl.loop(0, NY)
        def _(k):
            peer = k * NC + 1 - c
            wait_in(buf.at[peer], rs.at[peer])

    local_copies[1].wait()
    local_copies[4].wait()
    gather_rest(wp_v, wp_rs, fp_ss)
    for i in range(PD // 2):
        hidden = jnp.tanh(
            jnp.dot(
                p_v[i * 2 * PL : (i + 1) * 2 * PL, :],
                wp_v[...].reshape(D, D),
                preferred_element_type=F32,
            )
        )
        for j in range(2):
            mean = jnp.sum(hidden[j * PL : (j + 1) * PL], axis=0, keepdims=True) * (1.0 / PL)
            p = i * 2 + j
            for b in range(8):
                emb_f[b * PD + p : b * PD + p + 1, :] = mean[:, b * 128 : (b + 1) * 128]
    emb = emb_f[...].astype(BF)
    emb_s[...] = emb
    emb_l[s] = emb
    local(emb_s, emb_hbm, 8).start()

    @pl.loop(1, NZ)
    def _(k):
        zz = (z + k) % NZ
        remote(emb_s, emb_l.at[s], emb_ss.at[k], emb_rs.at[z], g, x * NZ + zz).start()

    send_rows(2, 0)
    send_rows(2, 1)

    local_copies[2].wait()
    gather_rest(ww_v, ww_rs, fw_ss)

    @pl.loop(1, NZ)
    def _(k):
        zz = (z + k) % NZ
        wait_in(emb_l.at[x * NZ + zz], emb_rs.at[zz])

    line = emb_l.at[pl.ds(x * NZ, NZ)]

    @pl.loop(1, NX)
    def _(k):
        xx = (x + k) % NX
        remote(line, line, line_ss.at[k], line_rs.at[x], g, xx * NZ + z).start()

    send_rows(3, 0)
    send_rows(3, 1)

    @pl.loop(0, TOK // 256)
    def _(i):
        at = pl.multiple_of(i * 256, 256)
        hidden = jnp.tanh(
            jnp.dot(x_v[pl.ds(at, 256), :], ww_v[...].reshape(D, D), preferred_element_type=F32)
        )
        d1_v[pl.ds(at, 256), :] = 1.0 - hidden * hidden
        q_at = pl.multiple_of(i * 8, 8)
        qv_f[pl.ds(q_at, 8), :] = jnp.sum(hidden.reshape(8, QL, D), axis=1) * (1.0 / QL)

    qv_v[...] = qv_f[...].astype(BF)

    def score(i):
        xx = (x + NX - i) % NX

        @pl.loop(0, NZ)
        def _(k):
            o = xx * NZ + (z + NZ + NZ - 1 - k) % NZ

            @pl.when(o != s)
            def _():
                wait_in(answer.at[o], row_rs.at[o])

        got = answer[pl.ds(xx * NZ, NZ)].reshape(NZ * CAP, D)
        s_v[:, pl.ds(pl.multiple_of(xx * NZ * CAP, NZ * CAP), NZ * CAP)] = lax.dot_general(
            qv_v[...], got, nt, preferred_element_type=F32
        )

    pl.loop(0, NX - 1)(score)

    @pl.loop(1, NX)
    def _(k):
        xx = (x + k) % NX
        wait_in(emb_l.at[pl.ds(xx * NZ, NZ)], line_rs.at[xx])

    pieces = emb_l[...].reshape(NS * 32, 128)
    to_passage, from_piece = iota((128, NS * 32), 0), iota((128, NS * 32), 1)
    for b in range(8):
        pick = (from_piece == (to_passage // PD) * 32 + b * PD + to_passage % PD)
        e_v[:, b * 128 : (b + 1) * 128] = jnp.dot(
            pick.astype(F32).astype(BF), pieces, preferred_element_type=F32
        ).astype(BF)

    in_logits = (
        lax.dot_general(qv_v[...], e_v[...], nt, preferred_element_type=F32) / logit_divisor
    )

    score(NX - 1)
    named = mask_v[...] > 0.5
    neg_logits = jnp.where(named, s_v[...] / logit_divisor, -jnp.inf)
    top = jnp.maximum(
        jnp.max(in_logits, axis=1, keepdims=True), jnp.max(neg_logits, axis=1, keepdims=True)
    )
    in_exp = jnp.exp(in_logits - top)
    neg_exp = jnp.where(named, jnp.exp(neg_logits - top), 0.0)
    total = jnp.sum(in_exp, axis=1, keepdims=True) + jnp.sum(neg_exp, axis=1, keepdims=True)
    label = (iota((QD, 128), 1) == to_column(pos_ref[...].astype(F32), QD).astype(jnp.int32))
    label = label.astype(F32)
    picked = jnp.sum(in_logits * label, axis=1, keepdims=True)
    loss_v[...] = to_row(jnp.log(total) + top - picked, QD)
    local(loss_v, loss_hbm, 9).start()
    coeff_in = (in_exp / total - label).astype(BF)
    coeff_neg = (neg_exp / total).astype(BF)
    query_grad = jnp.dot(coeff_in, e_v[...], preferred_element_type=F32) + jnp.dot(
        coeff_neg, answer[...].reshape(SLOTS, D), preferred_element_type=F32
    )
    qg_v[...] = query_grad * GRAD_SCALE * (1.0 / QL)

    def gradient_of_hidden(half):
        columns = pl.ds(pl.multiple_of(half * (D // 2), D // 2), D // 2)

        @pl.loop(0, QD // 8)
        def _(i):
            grads = qg_v[pl.ds(pl.multiple_of(i * 8, 8), 8), columns]
            for j in range(8):
                at = pl.ds(pl.multiple_of(i * 256 + j * QL, QL), QL)
                hg_v[half, at, :] = (d1_v[at, columns] * grads[j : j + 1, :]).astype(BF)

    gradient_of_hidden(1 - c)

    def turn(i):
        return (x + 2 - i + 3 * (i // 2) + 2 * (i // 3)) % NX

    def finish(i):
        xx = turn(i)
        wait_in(ex_l.at[i], ex_rs.at[i])
        both = own_v[i % 2] + ex_l[i].astype(F32)
        part_a, part_b = both[:RA], both[RA:]
        acc_b[xx] = part_b
        b_s[xx] = part_b.astype(BF)
        for k in range(NY):
            piece = part_a[:, k * 128 : (k + 1) * 128]
            acc_a[k, xx] = piece
            a_s[k, xx] = piece.astype(BF)

        @pl.when(i < NX - 1)
        def _():
            remote(b_s.at[xx], b_l.at[i], b_ss.at[i], b_rs.at[i], g, xx * NZ + z).start()

        @pl.loop(1, NY)
        def _(k):
            yy = (y + k) % NY
            remote(
                a_s.at[yy, xx], a_l.at[k - 1, xx], a_ss.at[k - 1, i], a_rs.at[k - 1, i],
                yy * NC + c, s,
            ).start()

    @pl.loop(0, NX)
    def _(i):
        xx = turn(i)
        left = xt_v[pl.ds(pl.multiple_of(xx * 256, 256), 256), :]
        ex_s[i] = jnp.dot(left, hg_v[1 - c], preferred_element_type=F32).astype(BF)
        remote(ex_s.at[i], ex_l.at[i], ex_ss.at[i], ex_rs.at[i], sib, s).start()

        @pl.when(i == 0)
        def _():
            gradient_of_hidden(c)

        @pl.when(i > 0)
        def _():
            finish(i - 1)

        own_v[i % 2] = jnp.dot(left, hg_v[c], preferred_element_type=F32)

    finish(NX - 1)

    def second_a(i, own=False):
        xx = turn(i)
        part = acc_a[y, xx]
        for k in range(1, NY):
            wait_in(a_l.at[k - 1, xx], a_rs.at[k - 1, i])
            part = part + a_l[k - 1, xx].astype(F32)
        part = part.reshape(ZA, 32, 128)
        za_s[xx] = part.astype(BF)

        if own:
            za_o[...] = part

        for zz in range(ZA):

            def send():
                remote(
                    za_s.at[xx, zz], z_l.at[s], za_ss.at[xx, zz], z_rs.at[s], g, xx * NZ + zz
                ).start()

            if own:
                pl.when(zz != z)(send)
            else:
                send()

    @pl.loop(0, NX - 1)
    def _(i):
        second_a(i)

    part_b = acc_b[x]
    for k in range(NX - 1):
        wait_in(b_l.at[k], b_rs.at[k])
        part_b = part_b + b_l[k].astype(F32)
    for k in range(NY):
        piece = part_b[:, k * 128 : (k + 1) * 128].reshape(ZB, 32, 128)
        zb_o[k] = piece
        zb_s[k] = piece.astype(BF)

    for k in range(NY):
        yy = (y + 1 + k) % NY
        for j in range(ZB):

            def send():
                remote(
                    zb_s.at[yy, j], z_l.at[y * NZ + z], zb_ss.at[yy, j], z_rs.at[y * NZ + z],
                    yy * NC + c, x * NZ + ZA + j,
                ).start()

            if k == NY - 1:
                pl.when(z != ZA + j)(send)
            else:
                send()

    second_a(NX - 1, own=True)

    @pl.loop(1, NS)
    def _(k):
        o = (s + k) % NS
        wait_out(req_s.at[o], req_ss.at[o])
        wait_out(found.at[0, 0, 0], row_ss.at[o])

    @pl.loop(1, NZ)
    def _(k):
        wait_out(emb_s, emb_ss.at[k])

    @pl.loop(1, NX)
    def _(k):
        wait_out(emb_l.at[pl.ds(0, NZ)], line_ss.at[k])

    for buf, ss, fs in ((wp_v, wp_ss, fp_ss), (ww_v, ww_ss, fw_ss)):

        @pl.loop(0, NY)
        def _(k):
            wait_out(buf.at[g], ss.at[k])

        @pl.loop(1, NY)
        def _(k):
            wait_out(buf.at[((y + k) % NY) * NC + c], fs.at[k])

    @pl.loop(0, NX)
    def _(i):
        wait_out(ex_s.at[i], ex_ss.at[i])

        @pl.loop(0, NY - 1)
        def _(k):
            wait_out(a_s.at[0, 0], a_ss.at[k, i])

    @pl.loop(0, NX - 1)
    def _(i):
        wait_out(b_s.at[i], b_ss.at[i])

    def collect(me, own):
        @pl.loop(1, NS)
        def _(k):
            wait_in(z_l.at[(me + k) % NS], z_rs.at[(me + k) % NS])

        total_part = own
        for k in range(1, NS):
            total_part = total_part + z_l[(me + k) % NS].astype(F32)
        f_s[...] = total_part.astype(BF)

    @pl.when(z < ZA)
    def _():
        collect(x * NZ + z, za_o[z])

    @pl.when(z >= ZA)
    def _():
        collect(y * NZ + z, zb_o[y, z - ZA])

    f_l[g] = f_s[...]

    @pl.loop(1, NG)
    def _(k):
        gg = (g + k) % NG
        remote(f_s, f_l.at[g], f_ss.at[k], f_rs.at[g], gg, s).start()

    @pl.loop(0, NX)
    def _(i):
        @pl.loop(0, ZA)
        def _(k):
            @pl.when((i - x) * NZ + k - z != 0)
            def _():
                wait_out(za_s.at[i, k], za_ss.at[i, k])

        @pl.loop(0, ZB)
        def _(k):
            @pl.when((i - y) * NZ + ZA + k - z != 0)
            def _():
                wait_out(zb_s.at[i, k], zb_ss.at[i, k])

    @pl.loop(1, NG)
    def _(k):
        gg = (g + k) % NG
        wait_in(f_l.at[gg], f_rs.at[gg])

    local(f_l, grad_hbm, 10).start()

    @pl.loop(1, NG)
    def _(k):
        wait_out(f_s, f_ss.at[k])

    local(emb_s, emb_hbm, 8).wait()
    local(loss_v, loss_hbm, 9).wait()
    local(f_l, grad_hbm, 10).wait()


def hand_over(grad, loss, emb, grad_out, loss_out, emb_out):
    for y in range(NY):
        for c in range(NC):
            at = (c * NY + y) * 128
            grad_out[:, at : at + 128] = grad[y * NC + c].astype(F32)
    loss_out[...] = loss[...]
    parts = emb[...].astype(F32)
    for b in range(8):
        emb_out[:, b * 128 : (b + 1) * 128] = parts[b * PD : (b + 1) * PD, :].astype(BF)


def shards(
    query_states, passage_states, index_rows, weight, prev_weight, neg_owner, neg_row, positive
):
    vmem = pl.BlockSpec(memory_space=pltpu.VMEM)
    hbm = pl.BlockSpec(memory_space=pltpu.HBM)
    dma = pltpu.SemaphoreType.DMA
    half = D // 2
    scratch = [
        pltpu.VMEM((NEG, 1, QD), jnp.int32),
        pltpu.VMEM((NEG, QD), jnp.int32),
        pltpu.VMEM((1, QD), jnp.int32),
        pltpu.VMEM((1, QD), F32),
        pltpu.VMEM((TOK, D), BF),
        pltpu.VMEM((D, TOK), BF),
        pltpu.VMEM((PD * PL, D), BF),
        pltpu.VMEM((ROWS, D), BF),
        pltpu.VMEM((NG, D // NG, D), BF),
        pltpu.VMEM((NG, D // NG, D), BF),
        pltpu.VMEM((NS, 1, 128), F32),
        pltpu.VMEM((NS, 1, 128), F32),
        pltpu.VMEM((NX, 2, 4, CAP, D), BF),
        pltpu.VMEM((NS, CAP, D), BF),
        pltpu.VMEM((QD, SLOTS), F32),
        pltpu.VMEM((32, 128), F32),
        pltpu.VMEM((32, 128), BF),
        pltpu.VMEM((NS, 32, 128), BF),
        pltpu.VMEM((NS * PD, D), BF),
        pltpu.VMEM((TOK, D), F32),
        pltpu.VMEM((QD, D), F32),
        pltpu.VMEM((QD, D), BF),
        pltpu.VMEM((QD, SLOTS), F32),
        pltpu.VMEM((QD, D), F32),
        pltpu.VMEM((2, TOK, half), BF),
        pltpu.VMEM((NX, 256, half), BF),
        pltpu.VMEM((NX, 256, half), BF),
        pltpu.VMEM((2, 256, half), F32),
        pltpu.VMEM((NY, NX, RA, 128), F32),
        pltpu.VMEM((NX, RB, half), F32),
        pltpu.VMEM((NY, NX, RA, 128), BF),
        pltpu.VMEM((NX, RB, half), BF),
        pltpu.VMEM((NY - 1, NX, RA, 128), BF),
        pltpu.VMEM((NX - 1, RB, half), BF),
        pltpu.VMEM((NX, ZA, 32, 128), BF),
        pltpu.VMEM((NY, ZB, 32, 128), BF),
        pltpu.VMEM((ZA, 32, 128), F32),
        pltpu.VMEM((NY, ZB, 32, 128), F32),
        pltpu.VMEM((NS, 32, 128), BF),
        pltpu.VMEM((32, 128), BF),
        pltpu.VMEM((NG, 32, 128), BF),
        dma((11,)),
        dma((NS,)), dma((NS,)),
        dma((NS,)), dma((NS,)),
        dma((NY,)), dma((NG,)),
        dma((NY,)), dma((NG,)),
        dma((NY,)), dma((NY,)),
        dma((NZ,)), dma((NZ,)),
        dma((NX,)), dma((NX,)),
        dma((NX,)), dma((NX,)),
        dma((NY - 1, NX)), dma((NY - 1, NX)),
        dma((NX - 1,)), dma((NX - 1,)),
        dma((NX, ZA)), dma((NY, ZB)), dma((NS,)),
        dma((NG,)), dma((NG,)),
    ]
    grad, loss, emb = pl.pallas_call(
        kernel,
        out_shape=(
            jax.ShapeDtypeStruct((NG, 32, 128), BF),
            jax.ShapeDtypeStruct((1, QD), F32),
            jax.ShapeDtypeStruct((PD * 8, 128), BF),
        ),
        in_specs=[hbm] * 8,
        out_specs=(hbm, hbm, hbm),
        scratch_shapes=scratch,
        compiler_params=pltpu.CompilerParams(
            collective_id=0, has_side_effects=True, vmem_limit_bytes=60 << 20
        ),
        cost_estimate=pl.CostEstimate(
            flops=16 * 2**30, bytes_accessed=12 * 2**20, transcendentals=3 * 2**20
        ),
        name="retriever_step",
    )(
        neg_owner.transpose(1, 2, 0),
        neg_row.T,
        positive.reshape(1, QD),
        query_states.reshape(TOK, D),
        passage_states.reshape(PD * PL, D),
        index_rows,
        weight,
        prev_weight,
    )
    grad, loss, emb = pl.pallas_call(
        hand_over,
        out_shape=(
            jax.ShapeDtypeStruct((D // NS, D), F32),
            jax.ShapeDtypeStruct((1, QD), F32),
            jax.ShapeDtypeStruct((PD, D), BF),
        ),
        in_specs=[vmem] * 3,
        out_specs=(vmem, vmem, vmem),
        name="hand_over",
    )(grad, loss, emb)
    return grad, loss.reshape(QD), emb


def solution(mesh):
    return jax.shard_map(
        shards,
        mesh=mesh,
        in_specs=(
            P(("group", "shard"), None, None),
            P(("group", "shard"), None, None),
            P(("group", "shard"), None),
            P("group", None),
            P("group", None),
            P(("group", "shard"), None, None),
            P(("group", "shard"), None),
            P(("group", "shard")),
        ),
        out_specs=(P("shard", None), P(("group", "shard")), P(("group", "shard"), None)),
        check_vma=False,
    )
```

```python
import functools
import math

import jax
import jax.numpy as jnp
from jax import lax
from jax.experimental import pallas as pl
from jax.experimental.pallas import tpu as pltpu
from jax.sharding import PartitionSpec as P

MESH = pl.DeviceIdType.MESH
BF = jnp.bfloat16
F32 = jnp.float32

logit_divisor = 0.05

D = 1024
QD = 64
QL = 32
PD = 4
PL = 128
NEG = 8
ROWS = 2048
CAP = 32
NY, NC, NX, NZ = 4, 2, 4, 8
NG, NS = NY * NC, NX * NZ
TOK = QD * QL
SLOTS = NS * CAP
ZA, ZB = 4, 4
RA, RB = ZA * 32, ZB * 32
GRAD_SCALE = 1.0 / (logit_divisor * math.sqrt(QD * NS * NG))


def iota(shape, axis):
    return lax.broadcasted_iota(jnp.int32, shape, axis)


def to_column(row, n):
    eye = iota((n, n), 0) == iota((n, n), 1)
    return jnp.sum(jnp.where(eye, row, jnp.zeros_like(row)), axis=1, keepdims=True)


def to_row(column, n):
    eye = iota((n, n), 0) == iota((n, n), 1)
    return jnp.sum(jnp.where(eye, column, jnp.zeros_like(column)), axis=0, keepdims=True)


def kernel(
    owner_hbm, row_hbm, pos_hbm, x_hbm, p_hbm, idx_hbm, w_hbm, pw_hbm,
    grad_hbm, loss_hbm, emb_hbm,
    owner_ref, row_ref, pos_ref, loss_v, x_v, xt_v, p_v, idx_v, wp_v, ww_v,
    req_s, req_l, found, answer, mask_v,
    emb_f, emb_s, emb_l, e_v,
    d1_v, qv_f, qv_v, s_v, qg_v, hg_v,
    ex_s, ex_l, own_v, acc_a, acc_b, a_s, b_s, a_l, b_l,
    za_s, zb_s, za_o, zb_o, z_l, f_s, f_l,
    loc_sem, req_ss, req_rs, row_ss, row_rs, wp_ss, wp_rs, ww_ss, ww_rs,
    fp_ss, fw_ss, emb_ss, emb_rs, line_ss, line_rs, ex_ss, ex_rs, a_ss, a_rs, b_ss, b_rs,
    za_ss, zb_ss, z_rs, f_ss, f_rs,
):
    g, s = lax.axis_index("group"), lax.axis_index("shard")
    y, c = g // NC, g % NC
    x, z = s // NZ, s % NZ
    sib = y * NC + 1 - c

    def local(src, dst, k):
        return pltpu.make_async_copy(src, dst, loc_sem.at[k])

    def remote(src, dst, ss, rs, gg, sh):
        return pltpu.make_async_remote_copy(
            src_ref=src, dst_ref=dst, send_sem=ss, recv_sem=rs,
            device_id=(gg, sh), device_id_type=MESH,
        )

    def wait_in(dst, rs):
        remote(dst, dst, rs, rs, sib, s).wait_recv()

    def wait_out(src, ss):
        remote(src, src, ss, ss, sib, s).wait_send()

    nt = (((1,), (1,)), ((), ()))

    small_copies = [
        local(owner_hbm, owner_ref, 5),
        local(row_hbm, row_ref, 6),
        local(pos_hbm, pos_ref, 7),
    ]
    for copy in small_copies:
        copy.start()

    barrier = pltpu.get_barrier_semaphore()

    @pl.loop(1, NS)
    def _(k):
        pl.semaphore_signal(barrier, inc=1, device_id=(g, (s + k) % NS), device_id_type=MESH)

    @pl.loop(1, NG)
    def _(k):
        pl.semaphore_signal(barrier, inc=1, device_id=((g + k) % NG, s), device_id_type=MESH)

    local_copies = [
        local(idx_hbm, idx_v, 0),
        local(pw_hbm, wp_v.at[g], 1),
        local(w_hbm, ww_v.at[g], 2),
        local(x_hbm, x_v, 3),
        local(p_hbm, p_v, 4),
    ]
    for copy in local_copies:
        copy.start()

    for copy in small_copies:
        copy.wait()
    upper = (iota((QD, QD), 0) < iota((QD, QD), 1)).astype(F32).astype(BF)
    base = jnp.zeros((NS, 1), F32)
    requests = jnp.zeros((NS, 128), F32)
    slots = []
    for n in range(NEG):
        owner = owner_ref[n]
        hot = (iota((NS, QD), 0) == owner).astype(F32)
        hot_bf = hot.astype(BF)
        before = jnp.dot(hot_bf, upper, preferred_element_type=F32) + base
        rank = jnp.sum(hot * before, axis=0, keepdims=True).astype(jnp.int32)
        base = base + jnp.sum(hot, axis=1, keepdims=True)
        slots.append((owner * CAP + rank).astype(F32))
        row = row_ref[n : n + 1, :]
        here = iota((128, QD), 0) == rank + (s % 4) * CAP
        high = jnp.where(here, row // 16, 0).astype(F32).astype(BF)
        low = jnp.where(here, row % 16, 0).astype(F32).astype(BF)
        requests = requests + (
            16.0 * lax.dot_general(hot_bf, high, nt, preferred_element_type=F32)
            + lax.dot_general(hot_bf, low, nt, preferred_element_type=F32)
        )
    for o in range(NS):
        req_s[o] = requests[o : o + 1, :]

    pl.semaphore_wait(barrier, NS - 1 + NG - 1)

    @pl.loop(1, NS)
    def _(k):
        o = (x + k // NZ) % NX * NZ + (z + k) % NZ
        remote(req_s.at[o], req_l.at[s], req_ss.at[o], req_rs.at[s], g, o).start()

    req_l[s] = req_s[s]

    def spread(hbm, buf, ss, rs):

        @pl.loop(1, NY)
        def _(k):
            peer = ((y + k) % NY) * NC + c
            remote(hbm, buf.at[g], ss.at[k], rs.at[g], peer, s).start()

        remote(hbm, buf.at[g], ss.at[0], rs.at[g], sib, s).start()

    spread(pw_hbm, wp_v, wp_ss, wp_rs)

    local_copies[0].wait()
    row_lane = iota((128, ROWS), 1)

    sets = ((4, 1, 2, 7), (0, 5, 6, 3))

    def send_rows(i, half):
        for step in sets[half]:
            r = (x + i) % NX * NZ + (z + step) % NZ

            def send():
                remote(
                    found.at[i, half, r % 4], answer.at[s], row_ss.at[r], row_rs.at[s], g, r
                ).start()

            if step:
                send()
            else:
                pl.when(i > 0)(send)

    @pl.loop(0, NX)
    def _(i):
        for half in range(2):
            ids = jnp.zeros((1, 128), F32)
            for step in sets[half]:
                r = (x + i) % NX * NZ + (z + step) % NZ

                def wait():
                    wait_in(req_l.at[r], req_rs.at[r])

                if step:
                    wait()
                else:
                    pl.when(i > 0)(wait)
                ids = ids + req_l[r]
            column = to_column(ids, 128).astype(jnp.int32)
            hot = (row_lane == column).astype(F32).astype(BF)
            got = jnp.dot(hot, idx_v[...], preferred_element_type=F32).astype(BF)
            found[i, half] = got.reshape(4, CAP, D)

            @pl.when(i < NX // 2)
            def _():
                send_rows(i, half)

    answer[s] = found[0, 1, s % 4]
    spread(w_hbm, ww_v, ww_ss, ww_rs)

    slot_lane = iota((QD, SLOTS), 1)
    mask = jnp.zeros((QD, SLOTS), F32)
    for n in range(NEG):
        mask = mask + (slot_lane == to_column(slots[n], QD).astype(jnp.int32)).astype(F32)
    mask_v[...] = mask

    def gather_rest(buf, rs, fs):
        @pl.loop(1, NY)
        def _(k):
            peer = ((y + k) % NY) * NC + c
            wait_in(buf.at[peer], rs.at[peer])
            remote(buf.at[peer], buf.at[peer], fs.at[k], rs.at[peer], sib, s).start()

        @pl.loop(0, NY)
        def _(k):
            peer = k * NC + 1 - c
            wait_in(buf.at[peer], rs.at[peer])

    local_copies[1].wait()
    local_copies[4].wait()
    gather_rest(wp_v, wp_rs, fp_ss)
    for i in range(PD // 2):
        hidden = jnp.tanh(
            jnp.dot(
                p_v[i * 2 * PL : (i + 1) * 2 * PL, :],
                wp_v[...].reshape(D, D),
                preferred_element_type=F32,
            )
        )
        for j in range(2):
            mean = jnp.sum(hidden[j * PL : (j + 1) * PL], axis=0, keepdims=True) * (1.0 / PL)
            p = i * 2 + j
            for b in range(8):
                emb_f[b * PD + p : b * PD + p + 1, :] = mean[:, b * 128 : (b + 1) * 128]
    emb = emb_f[...].astype(BF)
    emb_s[...] = emb
    emb_l[s] = emb
    local(emb_s, emb_hbm, 8).start()

    @pl.loop(1, NZ)
    def _(k):
        zz = (z + k) % NZ
        remote(emb_s, emb_l.at[s], emb_ss.at[k], emb_rs.at[z], g, x * NZ + zz).start()

    send_rows(2, 0)
    send_rows(2, 1)
    send_rows(3, 0)

    local_copies[3].wait()
    local_copies[2].wait()
    gather_rest(ww_v, ww_rs, fw_ss)

    @pl.loop(1, NZ)
    def _(k):
        zz = (z + k) % NZ
        wait_in(emb_l.at[x * NZ + zz], emb_rs.at[zz])

    line = emb_l.at[pl.ds(x * NZ, NZ)]

    @pl.loop(1, NX)
    def _(k):
        xx = (x + k) % NX
        remote(line, line, line_ss.at[k], line_rs.at[x], g, xx * NZ + z).start()

    send_rows(3, 1)

    @pl.loop(0, TOK // 256)
    def _(i):
        at = pl.multiple_of(i * 256, 256)
        hidden = jnp.tanh(
            jnp.dot(x_v[pl.ds(at, 256), :], ww_v[...].reshape(D, D), preferred_element_type=F32)
        )
        d1_v[pl.ds(at, 256), :] = 1.0 - hidden * hidden
        q_at = pl.multiple_of(i * 8, 8)
        qv_f[pl.ds(q_at, 8), :] = jnp.sum(hidden.reshape(8, QL, D), axis=1) * (1.0 / QL)

    qv_v[...] = qv_f[...].astype(BF)

    @pl.loop(0, TOK // 256)
    def _(i):
        at = pl.multiple_of(i * 256, 256)
        xt_v[:, pl.ds(at, 256)] = x_v[pl.ds(at, 256), :].T

    def score(i):
        xx = (x + NX - i) % NX

        @pl.loop(0, NZ)
        def _(k):
            o = xx * NZ + (z + NZ + NZ - 1 - k) % NZ

            @pl.when(o != s)
            def _():
                wait_in(answer.at[o], row_rs.at[o])

        got = answer[pl.ds(xx * NZ, NZ)].reshape(NZ * CAP, D)
        s_v[:, pl.ds(pl.multiple_of(xx * NZ * CAP, NZ * CAP), NZ * CAP)] = lax.dot_general(
            qv_v[...], got, nt, preferred_element_type=F32
        )

    pl.loop(0, NX - 1)(score)

    @pl.loop(1, NX)
    def _(k):
        xx = (x + k) % NX
        wait_in(emb_l.at[pl.ds(xx * NZ, NZ)], line_rs.at[xx])

    pieces = emb_l[...].reshape(NS * 32, 128)
    to_passage, from_piece = iota((128, NS * 32), 0), iota((128, NS * 32), 1)
    for b in range(8):
        pick = (from_piece == (to_passage // PD) * 32 + b * PD + to_passage % PD)
        e_v[:, b * 128 : (b + 1) * 128] = jnp.dot(
            pick.astype(F32).astype(BF), pieces, preferred_element_type=F32
        ).astype(BF)

    in_logits = (
        lax.dot_general(qv_v[...], e_v[...], nt, preferred_element_type=F32) / logit_divisor
    )

    score(NX - 1)
    named = mask_v[...] > 0.5
    neg_logits = jnp.where(named, s_v[...] / logit_divisor, -jnp.inf)
    top = jnp.maximum(
        jnp.max(in_logits, axis=1, keepdims=True), jnp.max(neg_logits, axis=1, keepdims=True)
    )
    in_exp = jnp.exp(in_logits - top)
    neg_exp = jnp.where(named, jnp.exp(neg_logits - top), 0.0)
    total = jnp.sum(in_exp, axis=1, keepdims=True) + jnp.sum(neg_exp, axis=1, keepdims=True)
    label = (iota((QD, 128), 1) == to_column(pos_ref[...].astype(F32), QD).astype(jnp.int32))
    label = label.astype(F32)
    picked = jnp.sum(in_logits * label, axis=1, keepdims=True)
    loss_v[...] = to_row(jnp.log(total) + top - picked, QD)
    local(loss_v, loss_hbm, 9).start()
    coeff_in = (in_exp / total - label).astype(BF)
    coeff_neg = (neg_exp / total).astype(BF)
    query_grad = jnp.dot(coeff_in, e_v[...], preferred_element_type=F32) + jnp.dot(
        coeff_neg, answer[...].reshape(SLOTS, D), preferred_element_type=F32
    )
    qg_v[...] = query_grad * GRAD_SCALE * (1.0 / QL)

    def gradient_of_hidden(half):
        columns = pl.ds(pl.multiple_of(half * (D // 2), D // 2), D // 2)

        @pl.loop(0, QD // 8)
        def _(i):
            grads = qg_v[pl.ds(pl.multiple_of(i * 8, 8), 8), columns]
            for j in range(8):
                at = pl.ds(pl.multiple_of(i * 256 + j * QL, QL), QL)
                hg_v[half, at, :] = (d1_v[at, columns] * grads[j : j + 1, :]).astype(BF)

    gradient_of_hidden(1 - c)

    def turn(i):
        return (x + 2 - i + 3 * (i // 2) + 2 * (i // 3)) % NX

    def finish(i):
        xx = turn(i)
        wait_in(ex_l.at[i], ex_rs.at[i])
        both = own_v[i % 2] + ex_l[i].astype(F32)
        part_a, part_b = both[:RA], both[RA:]
        acc_b[xx] = part_b
        b_s[xx] = part_b.astype(BF)
        for k in range(NY):
            piece = part_a[:, k * 128 : (k + 1) * 128]
            acc_a[k, xx] = piece
            a_s[k, xx] = piece.astype(BF)

        @pl.when(i < NX - 1)
        def _():
            remote(b_s.at[xx], b_l.at[i], b_ss.at[i], b_rs.at[i], g, xx * NZ + z).start()

        @pl.loop(1, NY)
        def _(k):
            yy = (y + k) % NY
            remote(
                a_s.at[yy, xx], a_l.at[k - 1, xx], a_ss.at[k - 1, i], a_rs.at[k - 1, i],
                yy * NC + c, s,
            ).start()

    @pl.loop(0, NX)
    def _(i):
        xx = turn(i)
        left = xt_v[pl.ds(pl.multiple_of(xx * 256, 256), 256), :]
        ex_s[i] = jnp.dot(left, hg_v[1 - c], preferred_element_type=F32).astype(BF)
        remote(ex_s.at[i], ex_l.at[i], ex_ss.at[i], ex_rs.at[i], sib, s).start()

        @pl.when(i == 0)
        def _():
            gradient_of_hidden(c)

        @pl.when(i > 0)
        def _():
            finish(i - 1)

        own_v[i % 2] = jnp.dot(left, hg_v[c], preferred_element_type=F32)

    finish(NX - 1)

    def second_a(i, own=False):
        xx = turn(i)
        part = acc_a[y, xx]
        for k in range(1, NY):
            wait_in(a_l.at[k - 1, xx], a_rs.at[k - 1, i])
            part = part + a_l[k - 1, xx].astype(F32)
        part = part.reshape(ZA, 32, 128)
        za_s[xx] = part.astype(BF)

        if own:
            za_o[...] = part

        for zz in range(ZA):

            def send():
                remote(
                    za_s.at[xx, zz], z_l.at[s], za_ss.at[xx, zz], z_rs.at[s], g, xx * NZ + zz
                ).start()

            if own:
                pl.when(zz != z)(send)
            else:
                send()

    @pl.loop(0, NX - 1)
    def _(i):
        second_a(i)

    part_b = acc_b[x]
    for k in range(NX - 1):
        wait_in(b_l.at[k], b_rs.at[k])
        part_b = part_b + b_l[k].astype(F32)
    for k in range(NY):
        piece = part_b[:, k * 128 : (k + 1) * 128].reshape(ZB, 32, 128)
        zb_o[k] = piece
        zb_s[k] = piece.astype(BF)

    for k in range(NY):
        yy = (y + 1 + k) % NY
        for j in range(ZB):

            def send():
                remote(
                    zb_s.at[yy, j], z_l.at[y * NZ + z], zb_ss.at[yy, j], z_rs.at[y * NZ + z],
                    yy * NC + c, x * NZ + ZA + j,
                ).start()

            if k == NY - 1:
                pl.when(z != ZA + j)(send)
            else:
                send()

    second_a(NX - 1, own=True)

    @pl.loop(1, NS)
    def _(k):
        o = (s + k) % NS
        wait_out(req_s.at[o], req_ss.at[o])
        wait_out(found.at[0, 0, 0], row_ss.at[o])

    @pl.loop(1, NZ)
    def _(k):
        wait_out(emb_s, emb_ss.at[k])

    @pl.loop(1, NX)
    def _(k):
        wait_out(emb_l.at[pl.ds(0, NZ)], line_ss.at[k])

    for buf, ss, fs in ((wp_v, wp_ss, fp_ss), (ww_v, ww_ss, fw_ss)):

        @pl.loop(0, NY)
        def _(k):
            wait_out(buf.at[g], ss.at[k])

        @pl.loop(1, NY)
        def _(k):
            wait_out(buf.at[((y + k) % NY) * NC + c], fs.at[k])

    @pl.loop(0, NX)
    def _(i):
        wait_out(ex_s.at[i], ex_ss.at[i])

        @pl.loop(0, NY - 1)
        def _(k):
            wait_out(a_s.at[0, 0], a_ss.at[k, i])

    @pl.loop(0, NX - 1)
    def _(i):
        wait_out(b_s.at[i], b_ss.at[i])

    def collect(me, own):
        @pl.loop(1, NS)
        def _(k):
            wait_in(z_l.at[(me + k) % NS], z_rs.at[(me + k) % NS])

        total_part = own
        for k in range(1, NS):
            total_part = total_part + z_l[(me + k) % NS].astype(F32)
        f_s[...] = total_part.astype(BF)

    @pl.when(z < ZA)
    def _():
        collect(x * NZ + z, za_o[z])

    @pl.when(z >= ZA)
    def _():
        collect(y * NZ + z, zb_o[y, z - ZA])

    f_l[g] = f_s[...]

    for k in (4, 5, 3, 2, 6, 1, 7):
        remote(f_s, f_l.at[g], f_ss.at[k], f_rs.at[g], (g + k) % NG, s).start()

    @pl.loop(0, NX)
    def _(i):
        @pl.loop(0, ZA)
        def _(k):
            @pl.when((i - x) * NZ + k - z != 0)
            def _():
                wait_out(za_s.at[i, k], za_ss.at[i, k])

        @pl.loop(0, ZB)
        def _(k):
            @pl.when((i - y) * NZ + ZA + k - z != 0)
            def _():
                wait_out(zb_s.at[i, k], zb_ss.at[i, k])

    @pl.loop(1, NG)
    def _(k):
        gg = (g + k) % NG
        wait_in(f_l.at[gg], f_rs.at[gg])

    local(f_l, grad_hbm, 10).start()

    @pl.loop(1, NG)
    def _(k):
        wait_out(f_s, f_ss.at[k])

    local(emb_s, emb_hbm, 8).wait()
    local(loss_v, loss_hbm, 9).wait()
    local(f_l, grad_hbm, 10).wait()


def hand_over(grad, loss, emb, grad_out, loss_out, emb_out):
    for y in range(NY):
        for c in range(NC):
            at = (c * NY + y) * 128
            grad_out[:, at : at + 128] = grad[y * NC + c].astype(F32)
    loss_out[...] = loss[...]
    parts = emb[...].astype(F32)
    for b in range(8):
        emb_out[:, b * 128 : (b + 1) * 128] = parts[b * PD : (b + 1) * PD, :].astype(BF)


def shards(
    query_states, passage_states, index_rows, weight, prev_weight, neg_owner, neg_row, positive
):
    vmem = pl.BlockSpec(memory_space=pltpu.VMEM)
    hbm = pl.BlockSpec(memory_space=pltpu.HBM)
    dma = pltpu.SemaphoreType.DMA
    half = D // 2
    scratch = [
        pltpu.VMEM((NEG, 1, QD), jnp.int32),
        pltpu.VMEM((NEG, QD), jnp.int32),
        pltpu.VMEM((1, QD), jnp.int32),
        pltpu.VMEM((1, QD), F32),
        pltpu.VMEM((TOK, D), BF),
        pltpu.VMEM((D, TOK), BF),
        pltpu.VMEM((PD * PL, D), BF),
        pltpu.VMEM((ROWS, D), BF),
        pltpu.VMEM((NG, D // NG, D), BF),
        pltpu.VMEM((NG, D // NG, D), BF),
        pltpu.VMEM((NS, 1, 128), F32),
        pltpu.VMEM((NS, 1, 128), F32),
        pltpu.VMEM((NX, 2, 4, CAP, D), BF),
        pltpu.VMEM((NS, CAP, D), BF),
        pltpu.VMEM((QD, SLOTS), F32),
        pltpu.VMEM((32, 128), F32),
        pltpu.VMEM((32, 128), BF),
        pltpu.VMEM((NS, 32, 128), BF),
        pltpu.VMEM((NS * PD, D), BF),
        pltpu.VMEM((TOK, D), F32),
        pltpu.VMEM((QD, D), F32),
        pltpu.VMEM((QD, D), BF),
        pltpu.VMEM((QD, SLOTS), F32),
        pltpu.VMEM((QD, D), F32),
        pltpu.VMEM((2, TOK, half), BF),
        pltpu.VMEM((NX, 256, half), BF),
        pltpu.VMEM((NX, 256, half), BF),
        pltpu.VMEM((2, 256, half), F32),
        pltpu.VMEM((NY, NX, RA, 128), F32),
        pltpu.VMEM((NX, RB, half), F32),
        pltpu.VMEM((NY, NX, RA, 128), BF),
        pltpu.VMEM((NX, RB, half), BF),
        pltpu.VMEM((NY - 1, NX, RA, 128), BF),
        pltpu.VMEM((NX - 1, RB, half), BF),
        pltpu.VMEM((NX, ZA, 32, 128), BF),
        pltpu.VMEM((NY, ZB, 32, 128), BF),
        pltpu.VMEM((ZA, 32, 128), F32),
        pltpu.VMEM((NY, ZB, 32, 128), F32),
        pltpu.VMEM((NS, 32, 128), BF),
        pltpu.VMEM((32, 128), BF),
        pltpu.VMEM((NG, 32, 128), BF),
        dma((11,)),
        dma((NS,)), dma((NS,)),
        dma((NS,)), dma((NS,)),
        dma((NY,)), dma((NG,)),
        dma((NY,)), dma((NG,)),
        dma((NY,)), dma((NY,)),
        dma((NZ,)), dma((NZ,)),
        dma((NX,)), dma((NX,)),
        dma((NX,)), dma((NX,)),
        dma((NY - 1, NX)), dma((NY - 1, NX)),
        dma((NX - 1,)), dma((NX - 1,)),
        dma((NX, ZA)), dma((NY, ZB)), dma((NS,)),
        dma((NG,)), dma((NG,)),
    ]
    grad, loss, emb = pl.pallas_call(
        kernel,
        out_shape=(
            jax.ShapeDtypeStruct((NG, 32, 128), BF),
            jax.ShapeDtypeStruct((1, QD), F32),
            jax.ShapeDtypeStruct((PD * 8, 128), BF),
        ),
        in_specs=[hbm] * 8,
        out_specs=(hbm, hbm, hbm),
        scratch_shapes=scratch,
        compiler_params=pltpu.CompilerParams(
            collective_id=0, has_side_effects=True, vmem_limit_bytes=60 << 20
        ),
        cost_estimate=pl.CostEstimate(
            flops=16 * 2**30, bytes_accessed=12 * 2**20, transcendentals=3 * 2**20
        ),
        name="retriever_step",
    )(
        neg_owner.transpose(1, 2, 0),
        neg_row.T,
        positive.reshape(1, QD),
        query_states.reshape(TOK, D),
        passage_states.reshape(PD * PL, D),
        index_rows,
        weight,
        prev_weight,
    )
    grad, loss, emb = pl.pallas_call(
        hand_over,
        out_shape=(
            jax.ShapeDtypeStruct((D // NS, D), F32),
            jax.ShapeDtypeStruct((1, QD), F32),
            jax.ShapeDtypeStruct((PD, D), BF),
        ),
        in_specs=[vmem] * 3,
        out_specs=(vmem, vmem, vmem),
        name="hand_over",
    )(grad, loss, emb)
    return grad, loss.reshape(QD), emb


def solution(mesh):
    return jax.shard_map(
        shards,
        mesh=mesh,
        in_specs=(
            P(("group", "shard"), None, None),
            P(("group", "shard"), None, None),
            P(("group", "shard"), None),
            P("group", None),
            P("group", None),
            P(("group", "shard"), None, None),
            P(("group", "shard"), None),
            P(("group", "shard")),
        ),
        out_specs=(P("shard", None), P(("group", "shard")), P(("group", "shard"), None)),
        check_vma=False,
    )
```

```python
import functools
import math

import jax
import jax.numpy as jnp
from jax import lax
from jax.experimental import pallas as pl
from jax.experimental.pallas import tpu as pltpu
from jax.sharding import PartitionSpec as P

MESH = pl.DeviceIdType.MESH
BF = jnp.bfloat16
F32 = jnp.float32

logit_divisor = 0.05

D = 1024
QD = 64
QL = 32
PD = 4
PL = 128
NEG = 8
ROWS = 2048
CAP = 32
NY, NC, NX, NZ = 4, 2, 4, 8
NG, NS = NY * NC, NX * NZ
TOK = QD * QL
SLOTS = NS * CAP
ZA, ZB = 4, 4
RA, RB = ZA * 32, ZB * 32
GRAD_SCALE = 1.0 / (logit_divisor * math.sqrt(QD * NS * NG))


def iota(shape, axis):
    return lax.broadcasted_iota(jnp.int32, shape, axis)


def to_column(row, n):
    eye = iota((n, n), 0) == iota((n, n), 1)
    return jnp.sum(jnp.where(eye, row, jnp.zeros_like(row)), axis=1, keepdims=True)


def to_row(column, n):
    eye = iota((n, n), 0) == iota((n, n), 1)
    return jnp.sum(jnp.where(eye, column, jnp.zeros_like(column)), axis=0, keepdims=True)


def kernel(
    owner_hbm, row_hbm, pos_hbm, x_hbm, p_hbm, idx_hbm, w_hbm, pw_hbm,
    grad_hbm, loss_hbm, emb_hbm,
    owner_ref, row_ref, pos_ref, loss_v, x_v, xt_v, p_v, idx_v, wp_v, ww_v,
    req_s, req_l, found, answer, mask_v,
    emb_f, emb_s, emb_l, e_v,
    d1_v, qv_f, qv_v, s_v, qg_v, hg_v,
    ex_s, ex_l, own_v, acc_a, acc_b, a_s, b_s, a_l, b_l,
    za_s, zb_s, za_o, zb_o, z_l, f_s, f_l,
    loc_sem, req_ss, req_rs, row_ss, row_rs, wp_ss, wp_rs, ww_ss, ww_rs,
    fp_ss, fw_ss, emb_ss, emb_rs, line_ss, line_rs, ex_ss, ex_rs, a_ss, a_rs, b_ss, b_rs,
    za_ss, zb_ss, z_rs, f_ss, f_rs,
):
    g, s = lax.axis_index("group"), lax.axis_index("shard")
    y, c = g // NC, g % NC
    x, z = s // NZ, s % NZ
    sib = y * NC + 1 - c

    def local(src, dst, k):
        return pltpu.make_async_copy(src, dst, loc_sem.at[k])

    def remote(src, dst, ss, rs, gg, sh):
        return pltpu.make_async_remote_copy(
            src_ref=src, dst_ref=dst, send_sem=ss, recv_sem=rs,
            device_id=(gg, sh), device_id_type=MESH,
        )

    def wait_in(dst, rs):
        remote(dst, dst, rs, rs, sib, s).wait_recv()

    def wait_out(src, ss):
        remote(src, src, ss, ss, sib, s).wait_send()

    nt = (((1,), (1,)), ((), ()))

    small_copies = [
        local(owner_hbm, owner_ref, 5),
        local(row_hbm, row_ref, 6),
        local(pos_hbm, pos_ref, 7),
    ]
    for copy in small_copies:
        copy.start()

    barrier = pltpu.get_barrier_semaphore()

    @pl.loop(1, NS)
    def _(k):
        pl.semaphore_signal(barrier, inc=1, device_id=(g, (s + k) % NS), device_id_type=MESH)

    @pl.loop(1, NG)
    def _(k):
        pl.semaphore_signal(barrier, inc=1, device_id=((g + k) % NG, s), device_id_type=MESH)

    local_copies = [
        local(idx_hbm, idx_v, 0),
        local(pw_hbm, wp_v.at[g], 1),
        local(w_hbm, ww_v.at[g], 2),
        local(x_hbm, x_v, 3),
        local(p_hbm, p_v, 4),
    ]
    for copy in local_copies:
        copy.start()

    for copy in small_copies:
        copy.wait()
    upper = (iota((QD, QD), 0) < iota((QD, QD), 1)).astype(F32).astype(BF)
    base = jnp.zeros((NS, 1), F32)
    requests = jnp.zeros((NS, 128), F32)
    slots = []
    for n in range(NEG):
        owner = owner_ref[n]
        hot = (iota((NS, QD), 0) == owner).astype(F32)
        hot_bf = hot.astype(BF)
        before = jnp.dot(hot_bf, upper, preferred_element_type=F32) + base
        rank = jnp.sum(hot * before, axis=0, keepdims=True).astype(jnp.int32)
        base = base + jnp.sum(hot, axis=1, keepdims=True)
        slots.append((owner * CAP + rank).astype(F32))
        row = row_ref[n : n + 1, :]
        here = iota((128, QD), 0) == rank + (s % 4) * CAP
        high = jnp.where(here, row // 16, 0).astype(F32).astype(BF)
        low = jnp.where(here, row % 16, 0).astype(F32).astype(BF)
        requests = requests + (
            16.0 * lax.dot_general(hot_bf, high, nt, preferred_element_type=F32)
            + lax.dot_general(hot_bf, low, nt, preferred_element_type=F32)
        )
    for o in range(NS):
        req_s[o] = requests[o : o + 1, :]

    pl.semaphore_wait(barrier, NS - 1 + NG - 1)

    @pl.loop(1, NS)
    def _(k):
        o = (x + k // NZ) % NX * NZ + (z + k) % NZ
        remote(req_s.at[o], req_l.at[s], req_ss.at[o], req_rs.at[s], g, o).start()

    req_l[s] = req_s[s]

    def spread(hbm, buf, ss, rs):

        @pl.loop(1, NY)
        def _(k):
            peer = ((y + k) % NY) * NC + c
            remote(hbm, buf.at[g], ss.at[k], rs.at[g], peer, s).start()

        remote(hbm, buf.at[g], ss.at[0], rs.at[g], sib, s).start()

    spread(pw_hbm, wp_v, wp_ss, wp_rs)

    local_copies[0].wait()
    row_lane = iota((128, ROWS), 1)

    sets = ((4, 1, 2, 7), (0, 5, 6, 3))

    def send_rows(i, half):
        for step in sets[half]:
            r = (x + i) % NX * NZ + (z + step) % NZ

            def send():
                remote(
                    found.at[i, half, r % 4], answer.at[s], row_ss.at[r], row_rs.at[s], g, r
                ).start()

            if step:
                send()
            else:
                pl.when(i > 0)(send)

    @pl.loop(0, NX)
    def _(i):
        for half in range(2):
            ids = jnp.zeros((1, 128), F32)
            for step in sets[half]:
                r = (x + i) % NX * NZ + (z + step) % NZ

                def wait():
                    wait_in(req_l.at[r], req_rs.at[r])

                if step:
                    wait()
                else:
                    pl.when(i > 0)(wait)
                ids = ids + req_l[r]
            column = to_column(ids, 128).astype(jnp.int32)
            hot = (row_lane == column).astype(F32).astype(BF)
            got = jnp.dot(hot, idx_v[...], preferred_element_type=F32).astype(BF)
            found[i, half] = got.reshape(4, CAP, D)

            @pl.when(i < NX // 2)
            def _():
                send_rows(i, half)

    answer[s] = found[0, 1, s % 4]
    spread(w_hbm, ww_v, ww_ss, ww_rs)

    slot_lane = iota((QD, SLOTS), 1)
    mask = jnp.zeros((QD, SLOTS), F32)
    for n in range(NEG):
        mask = mask + (slot_lane == to_column(slots[n], QD).astype(jnp.int32)).astype(F32)
    mask_v[...] = mask

    def gather_rest(buf, rs, fs):
        @pl.loop(1, NY)
        def _(k):
            peer = ((y + k) % NY) * NC + c
            wait_in(buf.at[peer], rs.at[peer])
            remote(buf.at[peer], buf.at[peer], fs.at[k], rs.at[peer], sib, s).start()

        @pl.loop(0, NY)
        def _(k):
            peer = k * NC + 1 - c
            wait_in(buf.at[peer], rs.at[peer])

    local_copies[1].wait()
    local_copies[4].wait()
    gather_rest(wp_v, wp_rs, fp_ss)
    for i in range(PD // 2):
        hidden = jnp.tanh(
            jnp.dot(
                p_v[i * 2 * PL : (i + 1) * 2 * PL, :],
                wp_v[...].reshape(D, D),
                preferred_element_type=F32,
            )
        )
        for j in range(2):
            mean = jnp.sum(hidden[j * PL : (j + 1) * PL], axis=0, keepdims=True) * (1.0 / PL)
            p = i * 2 + j
            for b in range(8):
                emb_f[b * PD + p : b * PD + p + 1, :] = mean[:, b * 128 : (b + 1) * 128]
    emb = emb_f[...].astype(BF)
    emb_s[...] = emb
    emb_l[s] = emb
    local(emb_s, emb_hbm, 8).start()

    @pl.loop(1, NZ)
    def _(k):
        zz = (z + k) % NZ
        remote(emb_s, emb_l.at[s], emb_ss.at[k], emb_rs.at[z], g, x * NZ + zz).start()

    send_rows(2, 0)
    send_rows(2, 1)
    send_rows(3, 0)

    local_copies[3].wait()
    local_copies[2].wait()
    gather_rest(ww_v, ww_rs, fw_ss)

    @pl.loop(1, NZ)
    def _(k):
        zz = (z + k) % NZ
        wait_in(emb_l.at[x * NZ + zz], emb_rs.at[zz])

    line = emb_l.at[pl.ds(x * NZ, NZ)]

    @pl.loop(1, NX)
    def _(k):
        xx = (x + k) % NX
        remote(line, line, line_ss.at[k], line_rs.at[x], g, xx * NZ + z).start()

    send_rows(3, 1)

    @pl.loop(0, TOK // 256)
    def _(i):
        at = pl.multiple_of(i * 256, 256)
        hidden = jnp.tanh(
            jnp.dot(x_v[pl.ds(at, 256), :], ww_v[...].reshape(D, D), preferred_element_type=F32)
        )
        d1_v[pl.ds(at, 256), :] = 1.0 - hidden * hidden
        q_at = pl.multiple_of(i * 8, 8)
        qv_f[pl.ds(q_at, 8), :] = jnp.sum(hidden.reshape(8, QL, D), axis=1) * (1.0 / QL)

    qv_v[...] = qv_f[...].astype(BF)

    @pl.loop(0, TOK // 256)
    def _(i):
        at = pl.multiple_of(i * 256, 256)
        xt_v[:, pl.ds(at, 256)] = x_v[pl.ds(at, 256), :].T

    @pl.loop(1, NS)
    def _(k):
        o = (s + k) % NS
        wait_out(req_s.at[o], req_ss.at[o])

    for buf, ss, fs in ((wp_v, wp_ss, fp_ss), (ww_v, ww_ss, fw_ss)):

        @pl.loop(0, NY)
        def _(k):
            wait_out(buf.at[g], ss.at[k])

        @pl.loop(1, NY)
        def _(k):
            wait_out(buf.at[((y + k) % NY) * NC + c], fs.at[k])

    def score(i):
        xx = (x + NX - i) % NX

        @pl.loop(0, NZ)
        def _(k):
            o = xx * NZ + (z + NZ + NZ - 1 - k) % NZ

            @pl.when(o != s)
            def _():
                wait_in(answer.at[o], row_rs.at[o])

        got = answer[pl.ds(xx * NZ, NZ)].reshape(NZ * CAP, D)
        s_v[:, pl.ds(pl.multiple_of(xx * NZ * CAP, NZ * CAP), NZ * CAP)] = lax.dot_general(
            qv_v[...], got, nt, preferred_element_type=F32
        )

    pl.loop(0, NX - 1)(score)

    @pl.loop(1, NX)
    def _(k):
        xx = (x + k) % NX
        wait_in(emb_l.at[pl.ds(xx * NZ, NZ)], line_rs.at[xx])

    pieces = emb_l[...].reshape(NS * 32, 128)
    to_passage, from_piece = iota((128, NS * 32), 0), iota((128, NS * 32), 1)
    for b in range(8):
        pick = (from_piece == (to_passage // PD) * 32 + b * PD + to_passage % PD)
        e_v[:, b * 128 : (b + 1) * 128] = jnp.dot(
            pick.astype(F32).astype(BF), pieces, preferred_element_type=F32
        ).astype(BF)

    in_logits = (
        lax.dot_general(qv_v[...], e_v[...], nt, preferred_element_type=F32) / logit_divisor
    )

    score(NX - 1)
    named = mask_v[...] > 0.5
    neg_logits = jnp.where(named, s_v[...] / logit_divisor, -jnp.inf)
    top = jnp.maximum(
        jnp.max(in_logits, axis=1, keepdims=True), jnp.max(neg_logits, axis=1, keepdims=True)
    )
    in_exp = jnp.exp(in_logits - top)
    neg_exp = jnp.where(named, jnp.exp(neg_logits - top), 0.0)
    total = jnp.sum(in_exp, axis=1, keepdims=True) + jnp.sum(neg_exp, axis=1, keepdims=True)
    label = (iota((QD, 128), 1) == to_column(pos_ref[...].astype(F32), QD).astype(jnp.int32))
    label = label.astype(F32)
    picked = jnp.sum(in_logits * label, axis=1, keepdims=True)
    loss_v[...] = to_row(jnp.log(total) + top - picked, QD)
    local(loss_v, loss_hbm, 9).start()
    coeff_in = (in_exp / total - label).astype(BF)
    coeff_neg = (neg_exp / total).astype(BF)
    query_grad = jnp.dot(coeff_in, e_v[...], preferred_element_type=F32) + jnp.dot(
        coeff_neg, answer[...].reshape(SLOTS, D), preferred_element_type=F32
    )
    qg_v[...] = query_grad * GRAD_SCALE * (1.0 / QL)

    def gradient_of_hidden(half):
        columns = pl.ds(pl.multiple_of(half * (D // 2), D // 2), D // 2)

        @pl.loop(0, QD // 8)
        def _(i):
            grads = qg_v[pl.ds(pl.multiple_of(i * 8, 8), 8), columns]
            for j in range(8):
                at = pl.ds(pl.multiple_of(i * 256 + j * QL, QL), QL)
                hg_v[half, at, :] = (d1_v[at, columns] * grads[j : j + 1, :]).astype(BF)

    gradient_of_hidden(1 - c)

    def turn(i):
        return (x + 2 - i + 3 * (i // 2) + 2 * (i // 3)) % NX

    def finish(i):
        xx = turn(i)
        wait_in(ex_l.at[i], ex_rs.at[i])
        both = own_v[i % 2] + ex_l[i].astype(F32)
        part_a, part_b = both[:RA], both[RA:]
        acc_b[xx] = part_b
        b_s[xx] = part_b.astype(BF)

        @pl.when(i < NX - 1)
        def _():
            remote(b_s.at[xx], b_l.at[i], b_ss.at[i], b_rs.at[i], g, xx * NZ + z).start()

        for k in range(NY):
            piece = part_a[:, k * 128 : (k + 1) * 128]
            acc_a[k, xx] = piece
            a_s[k, xx] = piece.astype(BF)

        @pl.loop(1, NY)
        def _(k):
            yy = (y + k) % NY
            remote(
                a_s.at[yy, xx], a_l.at[k - 1, xx], a_ss.at[k - 1, i], a_rs.at[k - 1, i],
                yy * NC + c, s,
            ).start()

    @pl.loop(0, NX)
    def _(i):
        xx = turn(i)
        left = xt_v[pl.ds(pl.multiple_of(xx * 256, 256), 256), :]
        ex_s[i] = jnp.dot(left, hg_v[1 - c], preferred_element_type=F32).astype(BF)
        remote(ex_s.at[i], ex_l.at[i], ex_ss.at[i], ex_rs.at[i], sib, s).start()

        @pl.when(i == 0)
        def _():
            gradient_of_hidden(c)

        @pl.when(i > 0)
        def _():
            finish(i - 1)

        own_v[i % 2] = jnp.dot(left, hg_v[c], preferred_element_type=F32)

    finish(NX - 1)

    def second_a(i, own=False):
        xx = turn(i)
        part = acc_a[y, xx]
        for k in range(1, NY):
            wait_in(a_l.at[k - 1, xx], a_rs.at[k - 1, i])
            part = part + a_l[k - 1, xx].astype(F32)
        part = part.reshape(ZA, 32, 128)
        za_s[xx] = part.astype(BF)

        if own:
            za_o[...] = part

        for zz in range(ZA):

            def send():
                remote(
                    za_s.at[xx, zz], z_l.at[s], za_ss.at[xx, zz], z_rs.at[s], g, xx * NZ + zz
                ).start()

            if own:
                pl.when(zz != z)(send)
            else:
                send()

    @pl.loop(0, NX - 1)
    def _(i):
        second_a(i)

    part_b = acc_b[x]
    for k in range(NX - 1):
        wait_in(b_l.at[k], b_rs.at[k])
        part_b = part_b + b_l[k].astype(F32)
    for k in range(NY):
        piece = part_b[:, k * 128 : (k + 1) * 128].reshape(ZB, 32, 128)
        zb_o[k] = piece
        zb_s[k] = piece.astype(BF)

    for k in range(NY):
        yy = (y + 1 + k) % NY
        for j in range(ZB):

            def send():
                remote(
                    zb_s.at[yy, j], z_l.at[y * NZ + z], zb_ss.at[yy, j], z_rs.at[y * NZ + z],
                    yy * NC + c, x * NZ + ZA + j,
                ).start()

            if k == NY - 1:
                pl.when(z != ZA + j)(send)
            else:
                send()

    second_a(NX - 1, own=True)

    @pl.loop(1, NS)
    def _(k):
        o = (s + k) % NS
        wait_out(found.at[0, 0, 0], row_ss.at[o])

    @pl.loop(1, NZ)
    def _(k):
        wait_out(emb_s, emb_ss.at[k])

    @pl.loop(1, NX)
    def _(k):
        wait_out(emb_l.at[pl.ds(0, NZ)], line_ss.at[k])

    @pl.loop(0, NX)
    def _(i):
        wait_out(ex_s.at[i], ex_ss.at[i])

        @pl.loop(0, NY - 1)
        def _(k):
            wait_out(a_s.at[0, 0], a_ss.at[k, i])

    @pl.loop(0, NX - 1)
    def _(i):
        wait_out(b_s.at[i], b_ss.at[i])

    def collect(me, own):
        @pl.loop(1, NS)
        def _(k):
            wait_in(z_l.at[(me + k) % NS], z_rs.at[(me + k) % NS])

        total_part = own
        for k in range(1, NS):
            total_part = total_part + z_l[(me + k) % NS].astype(F32)
        f_s[...] = total_part.astype(BF)

    @pl.when(z < ZA)
    def _():
        collect(x * NZ + z, za_o[z])

    @pl.when(z >= ZA)
    def _():
        collect(y * NZ + z, zb_o[y, z - ZA])

    f_l[g] = f_s[...]

    for k in (4, 5, 3, 2, 6, 1, 7):
        remote(f_s, f_l.at[g], f_ss.at[k], f_rs.at[g], (g + k) % NG, s).start()

    @pl.loop(0, NX)
    def _(i):
        @pl.loop(0, ZA)
        def _(k):
            @pl.when((i - x) * NZ + k - z != 0)
            def _():
                wait_out(za_s.at[i, k], za_ss.at[i, k])

        @pl.loop(0, ZB)
        def _(k):
            @pl.when((i - y) * NZ + ZA + k - z != 0)
            def _():
                wait_out(zb_s.at[i, k], zb_ss.at[i, k])

    @pl.loop(1, NG)
    def _(k):
        gg = (g + k) % NG
        wait_in(f_l.at[gg], f_rs.at[gg])

    local(f_l, grad_hbm, 10).start()

    @pl.loop(1, NG)
    def _(k):
        wait_out(f_s, f_ss.at[k])

    local(emb_s, emb_hbm, 8).wait()
    local(loss_v, loss_hbm, 9).wait()
    local(f_l, grad_hbm, 10).wait()


def hand_over(grad, loss, emb, grad_out, loss_out, emb_out):
    for y in range(NY):
        for c in range(NC):
            at = (c * NY + y) * 128
            grad_out[:, at : at + 128] = grad[y * NC + c].astype(F32)
    loss_out[...] = loss[...]
    parts = emb[...].astype(F32)
    for b in range(8):
        emb_out[:, b * 128 : (b + 1) * 128] = parts[b * PD : (b + 1) * PD, :].astype(BF)


def shards(
    query_states, passage_states, index_rows, weight, prev_weight, neg_owner, neg_row, positive
):
    vmem = pl.BlockSpec(memory_space=pltpu.VMEM)
    hbm = pl.BlockSpec(memory_space=pltpu.HBM)
    dma = pltpu.SemaphoreType.DMA
    half = D // 2
    scratch = [
        pltpu.VMEM((NEG, 1, QD), jnp.int32),
        pltpu.VMEM((NEG, QD), jnp.int32),
        pltpu.VMEM((1, QD), jnp.int32),
        pltpu.VMEM((1, QD), F32),
        pltpu.VMEM((TOK, D), BF),
        pltpu.VMEM((D, TOK), BF),
        pltpu.VMEM((PD * PL, D), BF),
        pltpu.VMEM((ROWS, D), BF),
        pltpu.VMEM((NG, D // NG, D), BF),
        pltpu.VMEM((NG, D // NG, D), BF),
        pltpu.VMEM((NS, 1, 128), F32),
        pltpu.VMEM((NS, 1, 128), F32),
        pltpu.VMEM((NX, 2, 4, CAP, D), BF),
        pltpu.VMEM((NS, CAP, D), BF),
        pltpu.VMEM((QD, SLOTS), F32),
        pltpu.VMEM((32, 128), F32),
        pltpu.VMEM((32, 128), BF),
        pltpu.VMEM((NS, 32, 128), BF),
        pltpu.VMEM((NS * PD, D), BF),
        pltpu.VMEM((TOK, D), F32),
        pltpu.VMEM((QD, D), F32),
        pltpu.VMEM((QD, D), BF),
        pltpu.VMEM((QD, SLOTS), F32),
        pltpu.VMEM((QD, D), F32),
        pltpu.VMEM((2, TOK, half), BF),
        pltpu.VMEM((NX, 256, half), BF),
        pltpu.VMEM((NX, 256, half), BF),
        pltpu.VMEM((2, 256, half), F32),
        pltpu.VMEM((NY, NX, RA, 128), F32),
        pltpu.VMEM((NX, RB, half), F32),
        pltpu.VMEM((NY, NX, RA, 128), BF),
        pltpu.VMEM((NX, RB, half), BF),
        pltpu.VMEM((NY - 1, NX, RA, 128), BF),
        pltpu.VMEM((NX - 1, RB, half), BF),
        pltpu.VMEM((NX, ZA, 32, 128), BF),
        pltpu.VMEM((NY, ZB, 32, 128), BF),
        pltpu.VMEM((ZA, 32, 128), F32),
        pltpu.VMEM((NY, ZB, 32, 128), F32),
        pltpu.VMEM((NS, 32, 128), BF),
        pltpu.VMEM((32, 128), BF),
        pltpu.VMEM((NG, 32, 128), BF),
        dma((11,)),
        dma((NS,)), dma((NS,)),
        dma((NS,)), dma((NS,)),
        dma((NY,)), dma((NG,)),
        dma((NY,)), dma((NG,)),
        dma((NY,)), dma((NY,)),
        dma((NZ,)), dma((NZ,)),
        dma((NX,)), dma((NX,)),
        dma((NX,)), dma((NX,)),
        dma((NY - 1, NX)), dma((NY - 1, NX)),
        dma((NX - 1,)), dma((NX - 1,)),
        dma((NX, ZA)), dma((NY, ZB)), dma((NS,)),
        dma((NG,)), dma((NG,)),
    ]
    grad, loss, emb = pl.pallas_call(
        kernel,
        out_shape=(
            jax.ShapeDtypeStruct((NG, 32, 128), BF),
            jax.ShapeDtypeStruct((1, QD), F32),
            jax.ShapeDtypeStruct((PD * 8, 128), BF),
        ),
        in_specs=[hbm] * 8,
        out_specs=(hbm, hbm, hbm),
        scratch_shapes=scratch,
        compiler_params=pltpu.CompilerParams(
            collective_id=0, has_side_effects=True, vmem_limit_bytes=60 << 20
        ),
        cost_estimate=pl.CostEstimate(
            flops=16 * 2**30, bytes_accessed=12 * 2**20, transcendentals=3 * 2**20
        ),
        name="retriever_step",
    )(
        neg_owner.transpose(1, 2, 0),
        neg_row.T,
        positive.reshape(1, QD),
        query_states.reshape(TOK, D),
        passage_states.reshape(PD * PL, D),
        index_rows,
        weight,
        prev_weight,
    )
    grad, loss, emb = pl.pallas_call(
        hand_over,
        out_shape=(
            jax.ShapeDtypeStruct((D // NS, D), F32),
            jax.ShapeDtypeStruct((1, QD), F32),
            jax.ShapeDtypeStruct((PD, D), BF),
        ),
        in_specs=[vmem] * 3,
        out_specs=(vmem, vmem, vmem),
        name="hand_over",
    )(grad, loss, emb)
    return grad, loss.reshape(QD), emb


def solution(mesh):
    return jax.shard_map(
        shards,
        mesh=mesh,
        in_specs=(
            P(("group", "shard"), None, None),
            P(("group", "shard"), None, None),
            P(("group", "shard"), None),
            P("group", None),
            P("group", None),
            P(("group", "shard"), None, None),
            P(("group", "shard"), None),
            P(("group", "shard")),
        ),
        out_specs=(P("shard", None), P(("group", "shard")), P(("group", "shard"), None)),
        check_vma=False,
    )
```
